32 devices in a mesh: cfg: 2 (over x), section: 8 (over z, core), patch: 2 (over y).
Axes of the slice: x: 2, y: 2, z: 4, core: 2. Of those that a mesh axis runs over, the one named last changes fastest.
Arguments:
- latent: float32 [4, 16, 64], replicated, may hold values from -6 to 6
- w_in: bfloat16 [64, 2432], P(None, 'patch'), may hold values from -0.75 to 0.75
- modulation: float32 [8, 2, 3, 2432], P('section', 'cfg'), may hold values from -3 to 3
- w_qkv: bfloat16 [8, 3, 1536, 2432], P('section', None, 'patch'), may hold values from -0.125 to 0.125
- text_kv: bfloat16 [8, 2, 333, 24, 128], P('section', 'cfg', None, 'patch'), may hold values from -6 to 6
- stale_kv: bfloat16 [8, 2, 64, 24, 128], P('section', 'cfg', None, 'patch'), may hold values from -6 to 6
- w_out: bfloat16 [8, 1536, 2432], P('section', None, 'patch'), may hold values from -0.625 to 0.625
- w_final: bfloat16 [2432, 64], P('patch'), may hold values from -0.125 to 0.125
- guidance: float32 [1], replicated, may hold values from 3 to 7
- step_index: int32 [1], replicated, may hold values from 0 to 27
Outputs:
- next_latent: float32 [16, 256], P('patch', ('cfg', 'section'))
The draws below stay inside these ranges and needn't reach their ends.
All inputs are finite; a program needn't handle non-finite values.
Results may differ from the reference program's by a relative error of at most 0.013.
Values may be sent and summed in bfloat16 or wider, within the bound.
A program may use at most 64 MiB of HBM per device.

```python
import jax
import jax.numpy as jnp
from jax import lax

D = 2432
HEADS = 24
HEAD_DIM = 64
INNER = 1536
CHAN = 64
TXT = 333
MICRO = 4
MB = 16
IMG = 64
STEPS = 28
BLOCKS = 8


def draw_modulation(key, part):
    key = jax.random.fold_in(key, 11)
    key_shift, key_gate, key_sign = jax.random.split(key, 3)
    polarity = (2 * jax.random.randint(key_sign, (BLOCKS, 2, 1, D), 0, 2) - 1).astype(jnp.float32)
    shifts = jnp.clip(0.5 * jax.random.normal(key_shift, (BLOCKS, 2, 2, D), jnp.float32), -3.0, 3.0)
    magnitude = jax.random.uniform(key_gate, (BLOCKS, 2, 1, D), jnp.float32, 1.0, 3.0)
    return jnp.concatenate([shifts, polarity * magnitude], axis=2)


def shard_levels(own_key, extent, cuts, low, high):
    loudness = 1.0
    for dim, blocks in cuts:
        draws = jax.random.uniform(jax.random.fold_in(jax.random.fold_in(own_key, 6), dim), (blocks,), jnp.float32, low / len(cuts), high / len(cuts))
        loudness = loudness * jnp.repeat(jnp.exp(draws), extent[dim] // blocks).reshape((-1,) + (1,) * (len(extent) - 1 - dim))
    return loudness


def bell_draw(stream_key, extent, spread, limit, cuts=(), held_as=jnp.bfloat16):
    gain = shard_levels(stream_key, extent, cuts, -0.22, 0.18) if cuts else 1.0
    array = jax.random.normal(stream_key, extent, jnp.float32) * spread * gain
    return jnp.minimum(jnp.maximum(array, -limit), limit).astype(held_as)


def setup_inputs(seed: int = 0) -> dict:
    splits = jax.random.split(jax.random.key(seed), 11)
    latent = bell_draw(splits[0], (MICRO, MB, CHAN), 1.0, 6.0, (), jnp.float32)
    w_in = bell_draw(splits[1], (CHAN, D), CHAN ** -0.5, 0.75, ((1, 2),))
    modulation = draw_modulation(jax.random.fold_in(splits[10], 71), 0)
    w_qkv = bell_draw(splits[3], (BLOCKS, 3, INNER, D), D ** -0.5, 0.125, ((0, 8), (2, 2)))
    text_kv = bell_draw(splits[4], (BLOCKS, 2, TXT, HEADS, 2 * HEAD_DIM), 1.0, 6.0, ((0, 8), (1, 2), (3, 2)))
    stale_kv = bell_draw(splits[5], (BLOCKS, 2, IMG, HEADS, 2 * HEAD_DIM), 1.0, 6.0, ((0, 8), (1, 2), (3, 2)))
    w_out = bell_draw(splits[6], (BLOCKS, INNER, D), (INNER // 16) ** -0.5, 0.625, ((0, 8), (2, 2)))
    w_final = bell_draw(splits[7], (D, CHAN), D ** -0.5, 0.125, ((0, 2),))
    guidance = jnp.clip(jax.random.uniform(splits[8], (1,), jnp.float32, 3.0, 7.0), 3.0, 7.0)
    step_index = jax.random.randint(splits[9], (1,), 0, STEPS).astype(jnp.int32)
    return dict(latent=latent, w_in=w_in, modulation=modulation, w_qkv=w_qkv, text_kv=text_kv, stale_kv=stale_kv, w_out=w_out, w_final=w_final, guidance=guidance, step_index=step_index)


SHIFT_SIGMA = 3.0
EPS_NORM = 1e-06

def sigma_at(position):
    level = 1.0 - position.astype(jnp.float32) / STEPS
    return SHIFT_SIGMA * level / (1.0 + (SHIFT_SIGMA - 1.0) * level)

def rms_heads(values):
    shaped = values.astype(jnp.float32).reshape(values.shape[:-1] + (-1, HEAD_DIM))
    scaled = shaped * lax.rsqrt(lax.optimization_barrier(jnp.mean(shaped * shaped, axis=-1, keepdims=True)) + EPS_NORM)
    return scaled.astype(jnp.bfloat16)

def attend(queries, all_keys, all_values):
    scores = jnp.einsum('rhd,khd->hrk', queries.astype(jnp.float32), all_keys.astype(jnp.float32)) / HEAD_DIM ** 0.5
    weights_soft = jax.nn.softmax(scores, axis=-1).astype(jnp.bfloat16)
    attended = jnp.einsum('hrk,khd->rhd', weights_soft.astype(jnp.float32), all_values.astype(jnp.float32))
    return attended.astype(jnp.bfloat16).reshape(queries.shape[0], -1)

def reference(latent, w_in, modulation, w_qkv, text_kv, stale_kv, w_out, w_final, guidance, step_index):
    embedded = jnp.dot(latent.astype(jnp.bfloat16).reshape(-1, CHAN), w_in, preferred_element_type=jnp.float32)
    embedded = embedded.astype(jnp.bfloat16).reshape(MICRO, MB, D)
    zero_index = jnp.zeros((), jnp.int32)
    velocities = []
    for branch in range(2):

        def block_step(hidden, per_block):
            shifts, w_proj, text_pair, stale_pair, w_back = per_block

            def patch_step(buffer, items):
                rows_in, micro_index = items
                residual = rows_in.astype(jnp.float32)
                row_mean = lax.optimization_barrier(jnp.mean(residual, axis=-1, keepdims=True))
                row_var = lax.optimization_barrier(jnp.mean((residual - row_mean) ** 2, axis=-1, keepdims=True))
                normed = (residual - row_mean) * lax.rsqrt(row_var + EPS_NORM)
                normed = (normed * (1.0 + shifts[1]) + shifts[0]).astype(jnp.bfloat16)
                projected = lax.dot_general(normed, w_proj.reshape(3 * INNER, D), (((1,), (1,)), ((), ())), preferred_element_type=jnp.float32)
                projected = projected.astype(jnp.bfloat16).reshape(MB, 3, INNER)
                new_pair = jnp.concatenate([projected[:, 1].reshape(MB, HEADS, HEAD_DIM), projected[:, 2].reshape(MB, HEADS, HEAD_DIM)], axis=-1)
                buffer = lax.dynamic_update_slice(buffer, new_pair, (micro_index * MB, zero_index, zero_index))
                joined = jnp.concatenate([text_pair, buffer], axis=0)
                all_keys = rms_heads(joined[:, :, :HEAD_DIM].reshape(-1, INNER))
                all_values = joined[:, :, HEAD_DIM:]
                attended = attend(rms_heads(projected[:, 0]), all_keys, all_values)
                update = jnp.dot(attended, w_back, preferred_element_type=jnp.float32)
                return (buffer, (residual + shifts[2] * update).astype(jnp.bfloat16))
            final_buffer, outputs = lax.scan(patch_step, stale_pair, (hidden, jnp.arange(MICRO, dtype=jnp.int32)))
            return (outputs, None)
        last_hidden, unused = lax.scan(block_step, embedded, (modulation[:, branch], w_qkv, text_kv[:, branch], stale_kv[:, branch], w_out))
        velocity = jnp.dot(last_hidden.reshape(-1, D), w_final, preferred_element_type=jnp.float32)
        velocities.append(velocity.reshape(MICRO, MB, CHAN))
    guided = velocities[1] + guidance[0] * (velocities[0] - velocities[1])
    step_size = sigma_at(step_index[0] + 1) - sigma_at(step_index[0])
    result = latent + step_size * guided
    return jnp.transpose(result, (1, 0, 2)).reshape(MB, MICRO * CHAN)
```

```python
import functools

import jax
import jax.numpy as jnp
from jax import lax
from jax.experimental import pallas as pl
from jax.experimental.pallas import tpu as pltpu
from jax.sharding import PartitionSpec as P

HEAD_DIM = 64
STEPS = 28
SHIFT_SIGMA = 3.0
EPS_NORM = 1e-06
MESH = pl.DeviceIdType.MESH
BF16 = jnp.bfloat16
F32 = jnp.float32


def sigma_at(position):
    level = 1.0 - position.astype(F32) / STEPS
    return SHIFT_SIGMA * level / (1.0 + (SHIFT_SIGMA - 1.0) * level)


def patch_of(index, micro_count, batch_rows):
    patch = jnp.zeros_like(index)
    for m in range(1, micro_count):
        patch = patch + jnp.where(index >= m * batch_rows, 1, 0)
    return patch


def kernel(
    dims,
    latent_ref, w_in_ref, mod_ref, gate_ref, kv_ref, w_final_ref, guide_ref, w_qkv_hbm, w_out_hbm,
    out_ref,
    w_qkv, w_out, xbuf, xfull, normed, keys, values_t, mask_old, mask_new, att_t, att_all, newx,
    speed, speeds, guided,
    w_sem, wo_sem, e_send, x_send, x_recv, a_send, a_recv, v_send, v_recv, g_send, g_recv,
):
    branches, sections, patches, groups, micro_count, batch_rows, img, txt = dims
    b, s, p = lax.axis_index("cfg"), lax.axis_index("section"), lax.axis_index("patch")
    last = sections - 1
    rows, columns = newx.shape
    heads, old, _ = kv_ref.shape
    group_heads = heads // groups
    group_inner = group_heads * HEAD_DIM
    half = micro_count // branches

    def weight_copy(c, g):
        part = pl.ds(g * group_inner, group_inner)
        return pltpu.make_async_copy(w_qkv_hbm.at[c, part], w_qkv.at[c, part], w_sem.at[c, g])

    for g in range(groups):
        for c in range(3):
            weight_copy(c, g).start()
    out_copy = pltpu.make_async_copy(w_out_hbm, w_out, wo_sem)
    out_copy.start()

    others = [lax.rem(p + d, patches) for d in range(1, patches)]

    barrier = pltpu.get_barrier_semaphore()
    for q in others:
        pl.semaphore_signal(barrier, inc=1, device_id={"patch": q}, device_id_type=MESH)

    @pl.when(s > 0)
    def _():
        for q in range(patches):
            pl.semaphore_signal(
                barrier, inc=1, device_id={"section": s - 1, "patch": q}, device_id_type=MESH
            )

    @pl.when(s < last)
    def _():
        pl.semaphore_signal(barrier, inc=1, device_id={"section": last}, device_id_type=MESH)

    @pl.when(s == last)
    def _():
        for e in range(1, branches):
            for q in range(patches):
                pl.semaphore_signal(
                    barrier, inc=1, device_id={"cfg": lax.rem(b + e, branches), "patch": q},
                    device_id_type=MESH,
                )

    @pl.when(s < last)
    def _():
        pl.semaphore_wait(barrier, 2 * patches - 1)

    @pl.when(s == last)
    def _():
        pl.semaphore_wait(barrier, branches * patches - 1 + last)

    def x_copy(source, q, sems, target):
        return pltpu.make_async_remote_copy(
            src_ref=source, dst_ref=xbuf.at[p], send_sem=sems.at[q], recv_sem=x_recv.at[p],
            device_id=target, device_id_type=MESH,
        )

    def x_arrival(q):
        return pltpu.make_async_remote_copy(
            src_ref=newx, dst_ref=xbuf.at[q], send_sem=x_send.at[0], recv_sem=x_recv.at[q],
            device_id={"patch": others[0]}, device_id_type=MESH,
        )

    @pl.when(s == 0)
    def _():
        embedded = jnp.dot(latent_ref[...], w_in_ref[...], preferred_element_type=F32)
        xbuf[p] = embedded.astype(BF16)
        for q in others:
            x_copy(xbuf.at[p], q, e_send, {"patch": q}).start()

    row_patch = patch_of(lax.broadcasted_iota(jnp.int32, (old, rows), 1), micro_count, batch_rows)
    key_index = lax.broadcasted_iota(jnp.int32, (old, rows), 0)
    key_patch = patch_of(key_index, micro_count, batch_rows)
    is_text = (key_index >= img) & (key_index < img + txt)
    is_stale = (key_index < img) & (key_patch > row_patch)
    mask_old[...] = jnp.where(is_text | is_stale, 1.0, 0.0)
    row_patch = patch_of(lax.broadcasted_iota(jnp.int32, (rows, rows), 1), micro_count, batch_rows)
    key_patch = patch_of(lax.broadcasted_iota(jnp.int32, (rows, rows), 0), micro_count, batch_rows)
    mask_new[...] = jnp.where(key_patch <= row_patch, 1.0, 0.0)

    @pl.loop(0, heads)
    def _(h):
        pair = kv_ref[h].astype(F32)
        key = pair[:, :HEAD_DIM]
        scale = lax.rsqrt(jnp.mean(key * key, axis=-1, keepdims=True) + EPS_NORM)
        keys[h] = (key * scale).astype(BF16)
        values_t[h] = pair.T[HEAD_DIM:].astype(BF16)

    @pl.when(s == 0)
    def _():
        for q in others:
            x_arrival(q).wait_recv()

    @pl.when(s > 0)
    def _():
        for q in range(patches):
            x_arrival(q).wait_recv()

    for q in range(patches):
        xfull[:, q * columns : (q + 1) * columns] = xbuf[q].astype(F32)
    x = xfull[...]
    centred = x - jnp.mean(x, axis=-1, keepdims=True)
    var = jnp.mean(centred * centred, axis=-1, keepdims=True)
    unit = centred * lax.rsqrt(var + EPS_NORM)
    normed[...] = (unit * (1.0 + mod_ref[1:2]) + mod_ref[0:1]).astype(BF16)

    def att_copy(g, q):
        return pltpu.make_async_remote_copy(
            src_ref=att_all.at[p, g], dst_ref=att_all.at[p, g], send_sem=a_send.at[q, g],
            recv_sem=a_recv.at[p, g], device_id={"patch": q}, device_id_type=MESH,
        )

    def att_arrival(g, q):
        return pltpu.make_async_remote_copy(
            src_ref=att_all.at[q, g], dst_ref=att_all.at[q, g], send_sem=a_send.at[q, g],
            recv_sem=a_recv.at[q, g], device_id={"patch": q}, device_id_type=MESH,
        )

    for g in range(groups):
        projected = []
        for c in range(3):
            weight_copy(c, g).wait()
            product = lax.dot_general(
                w_qkv[c, g * group_inner : (g + 1) * group_inner], normed[...],
                (((1,), (1,)), ((), ())), preferred_element_type=F32,
            )
            projected.append(product.astype(BF16).reshape(group_heads, HEAD_DIM, rows))
        scaled = []
        for c in range(2):
            part = projected[c].astype(F32)
            scale = lax.rsqrt(jnp.mean(part * part, axis=1, keepdims=True) + EPS_NORM)
            scaled.append((part * scale).astype(BF16))
        for j in range(group_heads):
            h = g * group_heads + j
            query = scaled[0][j] * BF16(HEAD_DIM**-0.5)
            score_old = jnp.dot(keys[h], query, preferred_element_type=F32)
            score_new = lax.dot_general(
                scaled[1][j], query, (((0,), (0,)), ((), ())), preferred_element_type=F32
            )
            power_old = jnp.exp(score_old) * mask_old[...]
            power_new = jnp.exp(score_new) * mask_new[...]
            total = jnp.sum(power_old, axis=0, keepdims=True) + jnp.sum(
                power_new, axis=0, keepdims=True
            )
            share = 1.0 / total
            att = jnp.dot(values_t[h], (power_old * share).astype(BF16), preferred_element_type=F32)
            att += jnp.dot(
                projected[2][j], (power_new * share).astype(BF16), preferred_element_type=F32
            )
            att_t[j * HEAD_DIM : (j + 1) * HEAD_DIM] = att
        att_all[p, g] = att_t[...].T.astype(BF16)
        for q in others:
            att_copy(g, q).start()

    out_copy.wait()

    def out_part(q, g):
        start = pl.multiple_of(q * (groups * group_inner) + g * group_inner, group_inner)
        return jnp.dot(
            att_all[q, g], w_out[pl.ds(start, group_inner)], preferred_element_type=F32
        )

    update = out_part(p, 0)
    for g in range(1, groups):
        update += out_part(p, g)
    for g in range(groups):
        for q in others:
            att_arrival(g, q).wait_recv()
            update += out_part(q, g)
    newx[...] = (xbuf[p].astype(F32) + gate_ref[...] * update).astype(BF16)

    @pl.when(s < last)
    def _():
        for q in range(patches):
            x_copy(newx, q, x_send, {"section": s + 1, "patch": q}).start()

    def v_copy(e, q):
        return pltpu.make_async_remote_copy(
            src_ref=speed.at[pl.ds(e * half, half), q], dst_ref=speeds.at[b, p],
            send_sem=v_send.at[e, q], recv_sem=v_recv.at[b, p],
            device_id={"cfg": e, "patch": q}, device_id_type=MESH,
        )

    def v_arrival(e, q):
        return pltpu.make_async_remote_copy(
            src_ref=speed.at[pl.ds(0, half), q], dst_ref=speeds.at[e, q],
            send_sem=v_send.at[e, q], recv_sem=v_recv.at[e, q],
            device_id={"cfg": e, "patch": q}, device_id_type=MESH,
        )

    def g_copy(t):
        return pltpu.make_async_remote_copy(
            src_ref=guided, dst_ref=guided, send_sem=g_send.at[t], recv_sem=g_recv,
            device_id={"section": t}, device_id_type=MESH,
        )

    @pl.when(s == last)
    def _():
        partial = jnp.dot(newx[...], w_final_ref[...], preferred_element_type=F32)
        speed[...] = partial.reshape(speed.shape)
        peers = []
        for e in range(branches):
            for d in range(patches):
                if e or d:
                    peers.append((lax.rem(b + e, branches), lax.rem(p + d, patches)))
        for e, q in peers:
            v_copy(e, q).start()
        speeds[b, p] = speed[pl.ds(b * half, half), p]
        for e, q in peers:
            v_arrival(e, q).wait_recv()
        conditional = jnp.sum(speeds[0], axis=0)
        unconditional = jnp.sum(speeds[1], axis=0)
        guided[...] = unconditional + guide_ref[0] * (conditional - unconditional)
        for t in range(last):
            g_copy(t).start()
        for e, q in peers:
            v_copy(e, q).wait_send()
        for t in range(last):
            g_copy(t).wait_send()

    @pl.when(s == 0)
    def _():
        for q in others:
            x_copy(xbuf.at[p], q, e_send, {"patch": q}).wait_send()

    for g in range(groups):
        for q in others:
            att_copy(g, q).wait_send()

    @pl.when(s < last)
    def _():
        for q in range(patches):
            x_copy(newx, q, x_send, {"section": s + 1, "patch": q}).wait_send()
        g_copy(s).wait_recv()

    out_ref[...] = guided[...]


def on_device(
    latent, w_in, modulation, w_qkv, text_kv, stale_kv, w_out, w_final, guidance, step_index
):
    branches, sections = lax.axis_size("cfg"), lax.axis_size("section")
    patches = lax.axis_size("patch")
    b, s, p = lax.axis_index("cfg"), lax.axis_index("section"), lax.axis_index("patch")
    micro_count, batch_rows, chan = latent.shape
    rows = micro_count * batch_rows
    own_rows = batch_rows // patches
    columns = w_in.shape[1]
    width = columns * patches
    local_inner = w_qkv.shape[2]
    heads = local_inner // HEAD_DIM
    inner = w_out.shape[1]
    txt, img = text_kv.shape[2], stale_kv.shape[2]
    old = -(-(txt + img) // 16) * 16
    half = micro_count // branches
    groups = next(g for g in (3, 2, 1) if g == 1 or local_inner % (g * 128) == 0)
    group_inner = local_inner // groups

    joined = jnp.concatenate([stale_kv[0, 0], text_kv[0, 0]], axis=0)
    joined = jnp.pad(joined, ((0, old - txt - img), (0, 0), (0, 0)))
    kv = jnp.transpose(joined, (1, 0, 2))
    mod = modulation[0, 0]
    gate = lax.dynamic_slice_in_dim(mod[2:3], p * columns, columns, 1)

    dims = (branches, sections, patches, groups, micro_count, batch_rows, img, txt)
    vmem = pl.BlockSpec(memory_space=pltpu.VMEM)
    dma = pltpu.SemaphoreType.DMA
    guided = pl.pallas_call(
        functools.partial(kernel, dims),
        out_shape=jax.ShapeDtypeStruct((half, own_rows, chan), F32),
        in_specs=[vmem] * 6
        + [pl.BlockSpec(memory_space=pltpu.SMEM)]
        + [pl.BlockSpec(memory_space=pl.ANY)] * 2,
        out_specs=vmem,
        scratch_shapes=[
            pltpu.VMEM((3, local_inner, width), BF16),
            pltpu.VMEM((inner, columns), BF16),
            pltpu.VMEM((patches, rows, columns), BF16),
            pltpu.VMEM((rows, width), F32),
            pltpu.VMEM((rows, width), BF16),
            pltpu.VMEM((heads, old, HEAD_DIM), BF16),
            pltpu.VMEM((heads, HEAD_DIM, old), BF16),
            pltpu.VMEM((old, rows), F32),
            pltpu.VMEM((rows, rows), F32),
            pltpu.VMEM((group_inner, rows), F32),
            pltpu.VMEM((patches, groups, rows, group_inner), BF16),
            pltpu.VMEM((rows, columns), BF16),
            pltpu.VMEM((micro_count, patches, own_rows, chan), F32),
            pltpu.VMEM((branches, patches, half, own_rows, chan), F32),
            pltpu.VMEM((half, own_rows, chan), F32),
            dma((3, groups)),
            dma,
            dma((patches,)),
            dma((patches,)),
            dma((patches,)),
            dma((patches, groups)),
            dma((patches, groups)),
            dma((branches, patches)),
            dma((branches, patches)),
            dma((sections,)),
            dma,
        ],
        compiler_params=pltpu.CompilerParams(
            collective_id=0, has_side_effects=True, vmem_limit_bytes=48 * 1024 * 1024
        ),
    )(
        latent.astype(BF16).reshape(rows, chan), w_in, mod, gate, kv, w_final, guidance,
        w_qkv[0], w_out[0],
    )

    section_width = half * chan // sections
    flat_guided = jnp.transpose(guided, (1, 0, 2)).reshape(own_rows, half * chan)
    own_latent = lax.dynamic_slice(
        latent, (b * half, p * own_rows, 0), (half, own_rows, chan)
    )
    flat_latent = jnp.transpose(own_latent, (1, 0, 2)).reshape(own_rows, half * chan)
    step_size = sigma_at(step_index[0] + 1) - sigma_at(step_index[0])
    result = flat_latent + step_size * flat_guided
    return lax.dynamic_slice_in_dim(result, s * section_width, section_width, 1)


def solution(mesh):
    in_specs = (
        P(),
        P(None, "patch"),
        P("section", "cfg", None, None),
        P("section", None, "patch", None),
        P("section", "cfg", None, "patch", None),
        P("section", "cfg", None, "patch", None),
        P("section", None, "patch"),
        P("patch", None),
        P(),
        P(),
    )
    out_specs = P("patch", ("cfg", "section"))
    return jax.shard_map(
        on_device, mesh=mesh, in_specs=in_specs, out_specs=out_specs, check_vma=False
    )
```

```python
import functools

import jax
import jax.numpy as jnp
from jax import lax
from jax.experimental import pallas as pl
from jax.experimental.pallas import tpu as pltpu
from jax.sharding import PartitionSpec as P

HEAD_DIM = 64
STEPS = 28
SHIFT_SIGMA = 3.0
EPS_NORM = 1e-06
MESH = pl.DeviceIdType.MESH
BF16 = jnp.bfloat16
F32 = jnp.float32


def sigma_at(position):
    level = 1.0 - position.astype(F32) / STEPS
    return SHIFT_SIGMA * level / (1.0 + (SHIFT_SIGMA - 1.0) * level)


def patch_of(index, micro_count, batch_rows):
    patch = jnp.zeros_like(index)
    for m in range(1, micro_count):
        patch = patch + jnp.where(index >= m * batch_rows, 1, 0)
    return patch


def kernel(
    dims,
    latent_ref, w_in_ref, mod_ref, gate_ref, kv_ref, w_final_ref, guide_ref, w_qkv_hbm, w_out_hbm,
    out_ref,
    w_qkv, w_out, xbuf, xfull, normed, keys, values_t, mask_old, mask_new, att_all, newx,
    speed, speeds, guided,
    w_sem, wo_sem, e_send, x_send, x_recv, a_send, a_recv, v_send, v_recv, g_send, g_recv,
):
    branches, sections, patches, groups, micro_count, batch_rows, img, txt, out_turned = dims
    b, s, p = lax.axis_index("cfg"), lax.axis_index("section"), lax.axis_index("patch")
    last = sections - 1
    rows, columns = newx.shape
    heads, old, _ = kv_ref.shape
    group_heads = heads // groups
    group_inner = group_heads * HEAD_DIM
    half = micro_count // branches

    def weight_copy(c, g):
        part = pl.ds(g * group_inner, group_inner)
        return pltpu.make_async_copy(w_qkv_hbm.at[c, part], w_qkv.at[c, part], w_sem.at[c, g])

    for g in range(groups):
        for c in range(3):
            weight_copy(c, g).start()
    out_copy = pltpu.make_async_copy(w_out_hbm, w_out, wo_sem)
    out_copy.start()

    others = [lax.rem(p + d, patches) for d in range(1, patches)]

    barrier = pltpu.get_barrier_semaphore()
    for q in others:
        pl.semaphore_signal(barrier, inc=1, device_id={"patch": q}, device_id_type=MESH)

    @pl.when(s > 0)
    def _():
        for q in range(patches):
            pl.semaphore_signal(
                barrier, inc=1, device_id={"section": s - 1, "patch": q}, device_id_type=MESH
            )

    @pl.when(s < last)
    def _():
        pl.semaphore_signal(barrier, inc=1, device_id={"section": last}, device_id_type=MESH)

    @pl.when(s == last)
    def _():
        for e in range(1, branches):
            for q in range(patches):
                pl.semaphore_signal(
                    barrier, inc=1, device_id={"cfg": lax.rem(b + e, branches), "patch": q},
                    device_id_type=MESH,
                )

    @pl.when(s < last)
    def _():
        pl.semaphore_wait(barrier, 2 * patches - 1)

    @pl.when(s == last)
    def _():
        pl.semaphore_wait(barrier, branches * patches - 1 + last)

    def x_copy(source, q, sems, target):
        return pltpu.make_async_remote_copy(
            src_ref=source, dst_ref=xbuf.at[p], send_sem=sems.at[q], recv_sem=x_recv.at[p],
            device_id=target, device_id_type=MESH,
        )

    def x_arrival(q):
        return pltpu.make_async_remote_copy(
            src_ref=newx, dst_ref=xbuf.at[q], send_sem=x_send.at[0], recv_sem=x_recv.at[q],
            device_id={"patch": others[0]}, device_id_type=MESH,
        )

    @pl.when(s == 0)
    def _():
        embedded = jnp.dot(latent_ref[...], w_in_ref[...], preferred_element_type=F32)
        xbuf[p] = embedded.astype(BF16)
        for q in others:
            x_copy(xbuf.at[p], q, e_send, {"patch": q}).start()

    row_patch = patch_of(lax.broadcasted_iota(jnp.int32, (old, rows), 1), micro_count, batch_rows)
    key_index = lax.broadcasted_iota(jnp.int32, (old, rows), 0)
    key_patch = patch_of(key_index, micro_count, batch_rows)
    is_text = (key_index >= img) & (key_index < img + txt)
    is_stale = (key_index < img) & (key_patch > row_patch)
    mask_old[...] = jnp.where(is_text | is_stale, 1.0, 0.0)
    row_patch = patch_of(lax.broadcasted_iota(jnp.int32, (rows, rows), 1), micro_count, batch_rows)
    key_patch = patch_of(lax.broadcasted_iota(jnp.int32, (rows, rows), 0), micro_count, batch_rows)
    mask_new[...] = jnp.where(key_patch <= row_patch, 1.0, 0.0)

    @pl.loop(0, heads)
    def _(h):
        pair = kv_ref[h].astype(F32)
        key = pair[:, :HEAD_DIM]
        scale = lax.rsqrt(jnp.mean(key * key, axis=-1, keepdims=True) + EPS_NORM)
        keys[h] = (key * scale).astype(BF16)
        values_t[h] = pair.T[HEAD_DIM:].astype(BF16)

    @pl.when(s == 0)
    def _():
        for q in others:
            x_arrival(q).wait_recv()

    @pl.when(s > 0)
    def _():
        for q in range(patches):
            x_arrival(q).wait_recv()

    for q in range(patches):
        xfull[:, q * columns : (q + 1) * columns] = xbuf[q].astype(F32)
    x = xfull[...]
    centred = x - jnp.mean(x, axis=-1, keepdims=True)
    var = jnp.mean(centred * centred, axis=-1, keepdims=True)
    unit = centred * lax.rsqrt(var + EPS_NORM)
    normed[...] = (unit * (1.0 + mod_ref[1:2]) + mod_ref[0:1]).astype(BF16)

    def att_copy(g, q):
        return pltpu.make_async_remote_copy(
            src_ref=att_all.at[p, g], dst_ref=att_all.at[p, g], send_sem=a_send.at[q, g],
            recv_sem=a_recv.at[p, g], device_id={"patch": q}, device_id_type=MESH,
        )

    def att_arrival(g, q):
        return pltpu.make_async_remote_copy(
            src_ref=att_all.at[q, g], dst_ref=att_all.at[q, g], send_sem=a_send.at[q, g],
            recv_sem=a_recv.at[q, g], device_id={"patch": q}, device_id_type=MESH,
        )

    for g in range(groups):
        projected = []
        for c in range(3):
            weight_copy(c, g).wait()
            product = lax.dot_general(
                w_qkv[c, g * group_inner : (g + 1) * group_inner], normed[...],
                (((1,), (1,)), ((), ())), preferred_element_type=F32,
            )
            projected.append(product.astype(BF16).reshape(group_heads, HEAD_DIM, rows))
        scaled = []
        for c in range(2):
            part = projected[c].astype(F32)
            scale = lax.rsqrt(jnp.mean(part * part, axis=1, keepdims=True) + EPS_NORM)
            scaled.append((part * scale).astype(BF16))
        scores = []
        for j in range(group_heads):
            query = scaled[0][j] * BF16(HEAD_DIM**-0.5)
            score_old = jnp.dot(keys[g * group_heads + j], query, preferred_element_type=F32)
            score_new = lax.dot_general(
                scaled[1][j], query, (((0,), (0,)), ((), ())), preferred_element_type=F32
            )
            scores.append((score_old, score_new))
        powers = [(jnp.exp(so) * mask_old[...], jnp.exp(sn) * mask_new[...]) for so, sn in scores]
        shares = [
            1.0 / (jnp.sum(po, axis=0, keepdims=True) + jnp.sum(pn, axis=0, keepdims=True))
            for po, pn in powers
        ]
        parts = []
        for j in range(group_heads):
            weights_old = (powers[j][0] * shares[j]).astype(BF16)
            weights_new = (powers[j][1] * shares[j]).astype(BF16)
            parts.append(
                jnp.dot(values_t[g * group_heads + j], weights_old, preferred_element_type=F32)
                + jnp.dot(projected[2][j], weights_new, preferred_element_type=F32)
            )
        att_all[p, g] = jnp.concatenate(parts, axis=0).T.astype(BF16)
        for q in others:
            att_copy(g, q).start()

    out_copy.wait()

    def out_part(q, g):
        start = pl.multiple_of(q * (groups * group_inner) + g * group_inner, group_inner)
        if out_turned:
            return lax.dot_general(
                att_all[q, g], w_out[:, pl.ds(start, group_inner)], (((1,), (1,)), ((), ())),
                preferred_element_type=F32,
            )
        return jnp.dot(
            att_all[q, g], w_out[pl.ds(start, group_inner)], preferred_element_type=F32
        )

    update = out_part(p, 0)
    for g in range(1, groups):
        update += out_part(p, g)
    for g in range(groups):
        for q in others:
            att_arrival(g, q).wait_recv()
            update += out_part(q, g)
    newx[...] = (xbuf[p].astype(F32) + gate_ref[...] * update).astype(BF16)

    @pl.when(s < last)
    def _():
        for q in range(patches):
            x_copy(newx, q, x_send, {"section": s + 1, "patch": q}).start()

    def v_copy(e, q):
        return pltpu.make_async_remote_copy(
            src_ref=speed.at[pl.ds(e * half, half), q], dst_ref=speeds.at[b, p],
            send_sem=v_send.at[e, q], recv_sem=v_recv.at[b, p],
            device_id={"cfg": e, "patch": q}, device_id_type=MESH,
        )

    def v_arrival(e, q):
        return pltpu.make_async_remote_copy(
            src_ref=speed.at[pl.ds(0, half), q], dst_ref=speeds.at[e, q],
            send_sem=v_send.at[e, q], recv_sem=v_recv.at[e, q],
            device_id={"cfg": e, "patch": q}, device_id_type=MESH,
        )

    def g_copy(t):
        return pltpu.make_async_remote_copy(
            src_ref=guided, dst_ref=guided, send_sem=g_send.at[t], recv_sem=g_recv,
            device_id={"section": t}, device_id_type=MESH,
        )

    @pl.when(s == last)
    def _():
        partial = lax.dot_general(
            newx[...], w_final_ref[...], (((1,), (1,)), ((), ())), preferred_element_type=F32
        )
        speed[...] = partial.reshape(speed.shape)
        peers = []
        for e in range(branches):
            for d in range(patches):
                if e or d:
                    peers.append((lax.rem(b + e, branches), lax.rem(p + d, patches)))
        for e, q in peers:
            v_copy(e, q).start()
        speeds[b, p] = speed[pl.ds(b * half, half), p]
        for e, q in peers:
            v_arrival(e, q).wait_recv()
        conditional = jnp.sum(speeds[0], axis=0)
        unconditional = jnp.sum(speeds[1], axis=0)
        guided[...] = unconditional + guide_ref[0] * (conditional - unconditional)
        for t in range(last):
            g_copy(t).start()
        for e, q in peers:
            v_copy(e, q).wait_send()
        for t in range(last):
            g_copy(t).wait_send()

    @pl.when(s == 0)
    def _():
        for q in others:
            x_copy(xbuf.at[p], q, e_send, {"patch": q}).wait_send()

    for g in range(groups):
        for q in others:
            att_copy(g, q).wait_send()

    @pl.when(s < last)
    def _():
        for q in range(patches):
            x_copy(newx, q, x_send, {"section": s + 1, "patch": q}).wait_send()
        g_copy(s).wait_recv()

    out_ref[...] = guided[...]


def on_device(
    latent, w_in, modulation, w_qkv, text_kv, stale_kv, w_out, w_final, guidance, step_index
):
    branches, sections = lax.axis_size("cfg"), lax.axis_size("section")
    patches = lax.axis_size("patch")
    b, s, p = lax.axis_index("cfg"), lax.axis_index("section"), lax.axis_index("patch")
    micro_count, batch_rows, chan = latent.shape
    rows = micro_count * batch_rows
    own_rows = batch_rows // patches
    columns = w_in.shape[1]
    width = columns * patches
    local_inner = w_qkv.shape[2]
    heads = local_inner // HEAD_DIM
    inner = w_out.shape[1]
    txt, img = text_kv.shape[2], stale_kv.shape[2]
    old = -(-(txt + img) // 16) * 16
    half = micro_count // branches
    groups = next(g for g in (3, 2, 1) if g == 1 or local_inner % (g * 128) == 0)
    group_inner = local_inner // groups

    joined = jnp.concatenate([stale_kv[0, 0], text_kv[0, 0]], axis=0)
    joined = jnp.pad(joined, ((0, old - txt - img), (0, 0), (0, 0)))
    kv = jnp.transpose(joined, (1, 0, 2))
    mod = modulation[0, 0]
    gate = lax.dynamic_slice_in_dim(mod[2:3], p * columns, columns, 1)

    out_turned = group_inner % 128 == 0
    dims = (
        branches, sections, patches, groups, micro_count, batch_rows, img, txt, out_turned
    )
    vmem = pl.BlockSpec(memory_space=pltpu.VMEM)
    dma = pltpu.SemaphoreType.DMA
    guided = pl.pallas_call(
        functools.partial(kernel, dims),
        out_shape=jax.ShapeDtypeStruct((half, own_rows, chan), F32),
        in_specs=[vmem] * 6
        + [pl.BlockSpec(memory_space=pltpu.SMEM)]
        + [pl.BlockSpec(memory_space=pl.ANY)] * 2,
        out_specs=vmem,
        scratch_shapes=[
            pltpu.VMEM((3, local_inner, width), BF16),
            pltpu.VMEM((columns, inner) if out_turned else (inner, columns), BF16),
            pltpu.VMEM((patches, rows, columns), BF16),
            pltpu.VMEM((rows, width), F32),
            pltpu.VMEM((rows, width), BF16),
            pltpu.VMEM((heads, old, HEAD_DIM), BF16),
            pltpu.VMEM((heads, HEAD_DIM, old), BF16),
            pltpu.VMEM((old, rows), F32),
            pltpu.VMEM((rows, rows), F32),
            pltpu.VMEM((patches, groups, rows, group_inner), BF16),
            pltpu.VMEM((rows, columns), BF16),
            pltpu.VMEM((micro_count, patches, own_rows, chan), F32),
            pltpu.VMEM((branches, patches, half, own_rows, chan), F32),
            pltpu.VMEM((half, own_rows, chan), F32),
            dma((3, groups)),
            dma,
            dma((patches,)),
            dma((patches,)),
            dma((patches,)),
            dma((patches, groups)),
            dma((patches, groups)),
            dma((branches, patches)),
            dma((branches, patches)),
            dma((sections,)),
            dma,
        ],
        compiler_params=pltpu.CompilerParams(
            collective_id=0, has_side_effects=True, vmem_limit_bytes=48 * 1024 * 1024
        ),
    )(
        latent.astype(BF16).reshape(rows, chan), w_in, mod, gate, kv, w_final.T, guidance,
        w_qkv[0], w_out[0].T if out_turned else w_out[0],
    )

    section_width = half * chan // sections
    flat_guided = jnp.transpose(guided, (1, 0, 2)).reshape(own_rows, half * chan)
    own_latent = lax.dynamic_slice(
        latent, (b * half, p * own_rows, 0), (half, own_rows, chan)
    )
    flat_latent = jnp.transpose(own_latent, (1, 0, 2)).reshape(own_rows, half * chan)
    step_size = sigma_at(step_index[0] + 1) - sigma_at(step_index[0])
    result = flat_latent + step_size * flat_guided
    return lax.dynamic_slice_in_dim(result, s * section_width, section_width, 1)


def solution(mesh):
    in_specs = (
        P(),
        P(None, "patch"),
        P("section", "cfg", None, None),
        P("section", None, "patch", None),
        P("section", "cfg", None, "patch", None),
        P("section", "cfg", None, "patch", None),
        P("section", None, "patch"),
        P("patch", None),
        P(),
        P(),
    )
    out_specs = P("patch", ("cfg", "section"))
    return jax.shard_map(
        on_device, mesh=mesh, in_specs=in_specs, out_specs=out_specs, check_vma=False
    )
```

```python
import functools

import jax
import jax.numpy as jnp
from jax import lax
from jax.experimental import pallas as pl
from jax.experimental.pallas import tpu as pltpu
from jax.sharding import PartitionSpec as P

HEAD_DIM = 64
STEPS = 28
SHIFT_SIGMA = 3.0
EPS_NORM = 1e-06
MESH = pl.DeviceIdType.MESH
BF16 = jnp.bfloat16
F32 = jnp.float32


def sigma_at(position):
    level = 1.0 - position.astype(F32) / STEPS
    return SHIFT_SIGMA * level / (1.0 + (SHIFT_SIGMA - 1.0) * level)


def patch_of(index, micro_count, batch_rows):
    patch = jnp.zeros_like(index)
    for m in range(1, micro_count):
        patch = patch + jnp.where(index >= m * batch_rows, 1, 0)
    return patch


def kernel(
    dims,
    latent_ref, w_in_ref, mod_ref, gate_ref, kv_ref, w_final_ref, guide_ref, w_qkv_hbm, w_out_hbm,
    out_ref,
    w_qkv, w_out, xbuf, xfull, normed, keys, values, key_mask, head_mask, att_all, newx,
    speed, speeds, guided,
    w_sem, wo_sem, e_send, x_send, x_recv, a_send, a_recv, v_send, v_recv, g_send, g_recv,
):
    branches, sections, patches, groups, micro_count, batch_rows, img, txt, out_turned = dims
    b, s, p = lax.axis_index("cfg"), lax.axis_index("section"), lax.axis_index("patch")
    last = sections - 1
    _, rows, columns = newx.shape
    heads, old, _ = kv_ref.shape
    group_heads = heads // groups
    group_inner = group_heads * HEAD_DIM
    half = micro_count // branches

    def weight_copy(c, g):
        part = pl.ds(g * group_inner, group_inner)
        return pltpu.make_async_copy(w_qkv_hbm.at[c, part], w_qkv.at[c, part], w_sem.at[c, g])

    for g in range(groups):
        for c in range(3):
            weight_copy(c, g).start()
    out_copy = pltpu.make_async_copy(w_out_hbm, w_out, wo_sem)
    out_copy.start()

    others = [lax.rem(p + d, patches) for d in range(1, patches)]

    barrier = pltpu.get_barrier_semaphore()
    for q in others:
        pl.semaphore_signal(barrier, inc=1, device_id={"patch": q}, device_id_type=MESH)

    @pl.when(s > 0)
    def _():
        for q in range(patches):
            pl.semaphore_signal(
                barrier, inc=1, device_id={"section": s - 1, "patch": q}, device_id_type=MESH
            )

    @pl.when(s < last)
    def _():
        pl.semaphore_signal(barrier, inc=1, device_id={"section": last}, device_id_type=MESH)

    @pl.when(s == last)
    def _():
        for e in range(1, branches):
            for q in range(patches):
                pl.semaphore_signal(
                    barrier, inc=1, device_id={"cfg": lax.rem(b + e, branches), "patch": q},
                    device_id_type=MESH,
                )

    @pl.when(s < last)
    def _():
        pl.semaphore_wait(barrier, 2 * patches - 1)

    @pl.when(s == last)
    def _():
        pl.semaphore_wait(barrier, branches * patches - 1 + last)

    def x_copy(source, f, q, sems, target):
        return pltpu.make_async_remote_copy(
            src_ref=source.at[f], dst_ref=xbuf.at[f, p], send_sem=sems.at[f, q],
            recv_sem=x_recv.at[f, p], device_id=target, device_id_type=MESH,
        )

    def embed_copy(f, q):
        return pltpu.make_async_remote_copy(
            src_ref=xbuf.at[f, p], dst_ref=xbuf.at[f, p], send_sem=e_send.at[f, q],
            recv_sem=x_recv.at[f, p], device_id={"patch": q}, device_id_type=MESH,
        )

    def x_arrival(f, q):
        return pltpu.make_async_remote_copy(
            src_ref=newx.at[f], dst_ref=xbuf.at[f, q], send_sem=x_send.at[f, 0],
            recv_sem=x_recv.at[f, q], device_id={"patch": others[0]}, device_id_type=MESH,
        )

    @pl.when(s == 0)
    def _():
        embedded = jnp.dot(latent_ref[...], w_in_ref[...], preferred_element_type=F32)
        embedded = embedded.astype(BF16).reshape(micro_count, rows, columns)
        for f in range(micro_count):
            xbuf[f, p] = embedded[f]
            for q in others:
                embed_copy(f, q).start()

    key_index = lax.broadcasted_iota(jnp.int32, key_mask.shape, 0)
    key_mask[...] = jnp.where(key_index < img + txt, 1.0, 0.0)
    row_head = patch_of(lax.broadcasted_iota(jnp.int32, head_mask.shape, 0), group_heads, rows)
    feature = lax.broadcasted_iota(jnp.int32, head_mask.shape, 1)
    feature_head = patch_of(feature, group_heads, HEAD_DIM)
    head_mask[...] = jnp.where(row_head == feature_head, 1.0, 0.0)
    turned_mask = head_mask[...].T

    @pl.loop(0, groups)
    def _(g):
        for j in range(group_heads):
            own = slice(j * HEAD_DIM, (j + 1) * HEAD_DIM)
            pair = kv_ref[g * group_heads + j].astype(F32)
            key = pair[:, :HEAD_DIM]
            scale = lax.rsqrt(jnp.mean(key * key, axis=-1, keepdims=True) + EPS_NORM)
            keys[g, :, own] = (key * scale).astype(BF16)
            values[g, :, own] = pair[:, HEAD_DIM:].astype(BF16)

    def att_copy(f, g, q):
        return pltpu.make_async_remote_copy(
            src_ref=att_all.at[f, p, g], dst_ref=att_all.at[f, p, g], send_sem=a_send.at[f, q, g],
            recv_sem=a_recv.at[f, p, g], device_id={"patch": q}, device_id_type=MESH,
        )

    def att_arrival(f, g, q):
        return pltpu.make_async_remote_copy(
            src_ref=att_all.at[f, q, g], dst_ref=att_all.at[f, q, g], send_sem=a_send.at[f, q, g],
            recv_sem=a_recv.at[f, q, g], device_id={"patch": q}, device_id_type=MESH,
        )

    def out_part(f, q, g):
        start = pl.multiple_of(q * (groups * group_inner) + g * group_inner, group_inner)
        if out_turned:
            return lax.dot_general(
                att_all[f, q, g], w_out[:, pl.ds(start, group_inner)], (((1,), (1,)), ((), ())),
                preferred_element_type=F32,
            )
        return jnp.dot(
            att_all[f, q, g], w_out[pl.ds(start, group_inner)], preferred_element_type=F32
        )

    @pl.loop(0, micro_count)
    def _(f):
        for q in range(patches):

            @pl.when((s > 0) | (p != q))
            def _():
                x_arrival(f, q).wait_recv()

        for q in range(patches):
            xfull[:, q * columns : (q + 1) * columns] = xbuf[f, q].astype(F32)
        x = xfull[...]
        centred = x - jnp.mean(x, axis=-1, keepdims=True)
        var = jnp.mean(centred * centred, axis=-1, keepdims=True)
        unit = centred * lax.rsqrt(var + EPS_NORM)
        unit = (unit * (1.0 + mod_ref[1:2]) + mod_ref[0:1]).astype(BF16)
        for j in range(group_heads):
            normed[j * rows : (j + 1) * rows] = unit
        own_rows = pl.ds(pl.multiple_of(f * rows, rows), rows)

        for g in range(groups):
            part = slice(g * group_inner, (g + 1) * group_inner)

            @pl.when(f == 0)
            def _():
                for c in range(3):
                    weight_copy(c, g).wait()

            turned = []
            for c in range(2):
                product = lax.dot_general(
                    w_qkv[c, part], normed[...] if c == 0 else normed[:rows],
                    (((1,), (1,)), ((), ())), preferred_element_type=F32,
                )
                product = product.astype(BF16).astype(F32)
                product = product.reshape(group_heads, HEAD_DIM, product.shape[-1])
                scale = lax.rsqrt(jnp.mean(product * product, axis=1, keepdims=True) + EPS_NORM)
                turned.append((product * scale).astype(BF16).astype(F32))
            value = lax.dot_general(
                normed[:rows], w_qkv[2, part], (((1,), (1,)), ((), ())), preferred_element_type=F32
            )
            keys[g, own_rows] = turned[1].reshape(group_inner, rows).T.astype(BF16)
            values[g, own_rows] = value.astype(BF16)
            query = turned[0].reshape(turned_mask.shape) * (turned_mask * HEAD_DIM**-0.5)
            scores = jnp.dot(keys[g], query.astype(BF16), preferred_element_type=F32)
            power = jnp.exp(scores) * key_mask[...]
            share = 1.0 / jnp.sum(power, axis=0, keepdims=True)
            att = lax.dot_general(
                (power * share).astype(BF16), values[g], (((0,), (0,)), ((), ())),
                preferred_element_type=F32,
            )
            att = (att * head_mask[...]).reshape(group_heads, rows, group_inner)
            att_all[f, p, g] = jnp.sum(att, axis=0).astype(BF16)
            for q in others:
                att_copy(f, g, q).start()

        @pl.when(f == 0)
        def _():
            out_copy.wait()

        update = out_part(f, p, 0)
        for g in range(1, groups):
            update += out_part(f, p, g)
        for g in range(groups):
            for q in others:
                att_arrival(f, g, q).wait_recv()
                update += out_part(f, q, g)
        newx[f] = (xbuf[f, p].astype(F32) + gate_ref[...] * update).astype(BF16)

        @pl.when(s < last)
        def _():
            for q in range(patches):
                x_copy(newx, f, q, x_send, {"section": s + 1, "patch": q}).start()

    def v_copy(e, q):
        return pltpu.make_async_remote_copy(
            src_ref=speed.at[pl.ds(e * half, half), q], dst_ref=speeds.at[b, p],
            send_sem=v_send.at[e, q], recv_sem=v_recv.at[b, p],
            device_id={"cfg": e, "patch": q}, device_id_type=MESH,
        )

    def v_arrival(e, q):
        return pltpu.make_async_remote_copy(
            src_ref=speed.at[pl.ds(0, half), q], dst_ref=speeds.at[e, q],
            send_sem=v_send.at[e, q], recv_sem=v_recv.at[e, q],
            device_id={"cfg": e, "patch": q}, device_id_type=MESH,
        )

    def g_copy(t):
        return pltpu.make_async_remote_copy(
            src_ref=guided, dst_ref=guided, send_sem=g_send.at[t], recv_sem=g_recv,
            device_id={"section": t}, device_id_type=MESH,
        )

    @pl.when(s == last)
    def _():
        partial = lax.dot_general(
            newx[...].reshape(micro_count * rows, columns), w_final_ref[...], (((1,), (1,)), ((), ())), preferred_element_type=F32
        )
        speed[...] = partial.reshape(speed.shape)
        peers = []
        for e in range(branches):
            for d in range(patches):
                if e or d:
                    peers.append((lax.rem(b + e, branches), lax.rem(p + d, patches)))
        for e, q in peers:
            v_copy(e, q).start()
        speeds[b, p] = speed[pl.ds(b * half, half), p]
        for e, q in peers:
            v_arrival(e, q).wait_recv()
        conditional = jnp.sum(speeds[0], axis=0)
        unconditional = jnp.sum(speeds[1], axis=0)
        guided[...] = unconditional + guide_ref[0] * (conditional - unconditional)
        for t in range(last):
            g_copy(t).start()
        for e, q in peers:
            v_copy(e, q).wait_send()
        for t in range(last):
            g_copy(t).wait_send()

    @pl.loop(0, micro_count)
    def _(f):
        @pl.when(s == 0)
        def _():
            for q in others:
                embed_copy(f, q).wait_send()

        for g in range(groups):
            for q in others:
                att_copy(f, g, q).wait_send()

        @pl.when(s < last)
        def _():
            for q in range(patches):
                x_copy(newx, f, q, x_send, {"section": s + 1, "patch": q}).wait_send()

    @pl.when(s < last)
    def _():
        g_copy(s).wait_recv()

    out_ref[...] = guided[...]


def on_device(
    latent, w_in, modulation, w_qkv, text_kv, stale_kv, w_out, w_final, guidance, step_index
):
    branches, sections = lax.axis_size("cfg"), lax.axis_size("section")
    patches = lax.axis_size("patch")
    b, s, p = lax.axis_index("cfg"), lax.axis_index("section"), lax.axis_index("patch")
    micro_count, batch_rows, chan = latent.shape
    rows = micro_count * batch_rows
    own_rows = batch_rows // patches
    columns = w_in.shape[1]
    width = columns * patches
    local_inner = w_qkv.shape[2]
    heads = local_inner // HEAD_DIM
    inner = w_out.shape[1]
    txt, img = text_kv.shape[2], stale_kv.shape[2]
    old = -(-(txt + img) // 16) * 16
    half = micro_count // branches
    groups = next(g for g in (3, 2, 1) if g == 1 or local_inner % (g * 128) == 0)
    group_inner = local_inner // groups
    tall = heads // groups * batch_rows

    joined = jnp.concatenate([stale_kv[0, 0], text_kv[0, 0]], axis=0)
    joined = jnp.pad(joined, ((0, old - txt - img), (0, 0), (0, 0)))
    kv = jnp.transpose(joined, (1, 0, 2))
    mod = modulation[0, 0]
    gate = lax.dynamic_slice_in_dim(mod[2:3], p * columns, columns, 1)

    out_turned = group_inner % 128 == 0
    dims = (
        branches, sections, patches, groups, micro_count, batch_rows, img, txt, out_turned
    )
    vmem = pl.BlockSpec(memory_space=pltpu.VMEM)
    dma = pltpu.SemaphoreType.DMA
    guided = pl.pallas_call(
        functools.partial(kernel, dims),
        out_shape=jax.ShapeDtypeStruct((half, own_rows, chan), F32),
        in_specs=[vmem] * 6
        + [pl.BlockSpec(memory_space=pltpu.SMEM)]
        + [pl.BlockSpec(memory_space=pl.ANY)] * 2,
        out_specs=vmem,
        scratch_shapes=[
            pltpu.VMEM((3, local_inner, width), BF16),
            pltpu.VMEM((columns, inner) if out_turned else (inner, columns), BF16),
            pltpu.VMEM((micro_count, patches, batch_rows, columns), BF16),
            pltpu.VMEM((batch_rows, width), F32),
            pltpu.VMEM((tall, width), BF16),
            pltpu.VMEM((groups, old, group_inner), BF16),
            pltpu.VMEM((groups, old, group_inner), BF16),
            pltpu.VMEM((old, tall), F32),
            pltpu.VMEM((tall, group_inner), F32),
            pltpu.VMEM((micro_count, patches, groups, batch_rows, group_inner), BF16),
            pltpu.VMEM((micro_count, batch_rows, columns), BF16),
            pltpu.VMEM((micro_count, patches, own_rows, chan), F32),
            pltpu.VMEM((branches, patches, half, own_rows, chan), F32),
            pltpu.VMEM((half, own_rows, chan), F32),
            dma((3, groups)),
            dma,
            dma((micro_count, patches)),
            dma((micro_count, patches)),
            dma((micro_count, patches)),
            dma((micro_count, patches, groups)),
            dma((micro_count, patches, groups)),
            dma((branches, patches)),
            dma((branches, patches)),
            dma((sections,)),
            dma,
        ],
        compiler_params=pltpu.CompilerParams(
            collective_id=0, has_side_effects=True, vmem_limit_bytes=48 * 1024 * 1024
        ),
    )(
        latent.astype(BF16).reshape(rows, chan), w_in, mod, gate, kv, w_final.T, guidance,
        w_qkv[0], w_out[0].T if out_turned else w_out[0],
    )

    section_width = half * chan // sections
    flat_guided = jnp.transpose(guided, (1, 0, 2)).reshape(own_rows, half * chan)
    own_latent = lax.dynamic_slice(
        latent, (b * half, p * own_rows, 0), (half, own_rows, chan)
    )
    flat_latent = jnp.transpose(own_latent, (1, 0, 2)).reshape(own_rows, half * chan)
    step_size = sigma_at(step_index[0] + 1) - sigma_at(step_index[0])
    result = flat_latent + step_size * flat_guided
    return lax.dynamic_slice_in_dim(result, s * section_width, section_width, 1)


def solution(mesh):
    in_specs = (
        P(),
        P(None, "patch"),
        P("section", "cfg", None, None),
        P("section", None, "patch", None),
        P("section", "cfg", None, "patch", None),
        P("section", "cfg", None, "patch", None),
        P("section", None, "patch"),
        P("patch", None),
        P(),
        P(),
    )
    out_specs = P("patch", ("cfg", "section"))
    return jax.shard_map(
        on_device, mesh=mesh, in_specs=in_specs, out_specs=out_specs, check_vma=False
    )
```

```python
import functools

import jax
import jax.numpy as jnp
from jax import lax
from jax.experimental import pallas as pl
from jax.experimental.pallas import tpu as pltpu
from jax.sharding import PartitionSpec as P

HEAD_DIM = 64
STEPS = 28
SHIFT_SIGMA = 3.0
EPS_NORM = 1e-06
MESH = pl.DeviceIdType.MESH
BF16 = jnp.bfloat16
F32 = jnp.float32


def sigma_at(position):
    level = 1.0 - position.astype(F32) / STEPS
    return SHIFT_SIGMA * level / (1.0 + (SHIFT_SIGMA - 1.0) * level)


def patch_of(index, micro_count, batch_rows):
    patch = jnp.zeros_like(index)
    for m in range(1, micro_count):
        patch = patch + jnp.where(index >= m * batch_rows, 1, 0)
    return patch


def kernel(
    dims,
    latent_ref, w_in_ref, mod_ref, text_ref, stale_ref, w_final_ref, guide_ref, w_qkv_hbm, w_out_hbm,
    out_ref,
    w_qkv, w_out, w_back, gate, xbuf, xfull, normed, keys, values, mask_old, mask_new, head_mask,
    att_all, newx,
    speed, speeds, guided,
    w_sem, wo_sem, e_send, x_send, x_recv, a_send, a_recv, v_send, v_recv, g_send, g_recv,
):
    branches, sections, patches, groups, micro_count, batch_rows, img, txt, out_turned = dims
    b, s, p = lax.axis_index("cfg"), lax.axis_index("section"), lax.axis_index("patch")
    last = sections - 1
    phases, rows, columns = newx.shape
    heads = text_ref.shape[0]
    old, tall = mask_old.shape[1:]
    per_phase = micro_count // phases
    group_heads = heads // groups
    group_inner = group_heads * HEAD_DIM
    half = micro_count // branches

    def weight_copy(c, g):
        part = pl.ds(g * group_inner, group_inner)
        return pltpu.make_async_copy(w_qkv_hbm.at[c, part], w_qkv.at[c, part], w_sem.at[c, g])

    for g in range(groups):
        for c in range(3):
            weight_copy(c, g).start()
    out_copy = pltpu.make_async_copy(w_out_hbm, w_out, wo_sem)
    out_copy.start()

    others = [lax.rem(p + d, patches) for d in range(1, patches)]

    barrier = pltpu.get_barrier_semaphore()
    for q in others:
        pl.semaphore_signal(barrier, inc=1, device_id={"patch": q}, device_id_type=MESH)

    @pl.when(s > 0)
    def _():
        for q in range(patches):
            pl.semaphore_signal(
                barrier, inc=1, device_id={"section": s - 1, "patch": q}, device_id_type=MESH
            )

    @pl.when(s < last)
    def _():
        pl.semaphore_signal(barrier, inc=1, device_id={"section": last}, device_id_type=MESH)

    @pl.when(s == last)
    def _():
        for e in range(1, branches):
            for q in range(patches):
                pl.semaphore_signal(
                    barrier, inc=1, device_id={"cfg": lax.rem(b + e, branches), "patch": q},
                    device_id_type=MESH,
                )

    @pl.when(s < last)
    def _():
        pl.semaphore_wait(barrier, 2 * patches - 1)

    @pl.when(s == last)
    def _():
        pl.semaphore_wait(barrier, branches * patches - 1 + last)

    def x_copy(source, f, q, sems, target):
        return pltpu.make_async_remote_copy(
            src_ref=source.at[f], dst_ref=xbuf.at[f, p], send_sem=sems.at[f, q],
            recv_sem=x_recv.at[f, p], device_id=target, device_id_type=MESH,
        )

    def embed_copy(f, q):
        return pltpu.make_async_remote_copy(
            src_ref=xbuf.at[f, p], dst_ref=xbuf.at[f, p], send_sem=e_send.at[f, q],
            recv_sem=x_recv.at[f, p], device_id={"patch": q}, device_id_type=MESH,
        )

    def x_arrival(f, q):
        return pltpu.make_async_remote_copy(
            src_ref=newx.at[f], dst_ref=xbuf.at[f, q], send_sem=x_send.at[f, 0],
            recv_sem=x_recv.at[f, q], device_id={"patch": others[0]}, device_id_type=MESH,
        )

    @pl.when(s == 0)
    def _():
        embedded = jnp.dot(latent_ref[...], w_in_ref[...], preferred_element_type=F32)
        embedded = embedded.astype(BF16).reshape(phases, rows, columns)
        for f in range(phases):
            xbuf[f, p] = embedded[f]
            for q in others:
                embed_copy(f, q).start()

    def row_patch_of(column):
        head = patch_of(column, group_heads, rows)
        return patch_of(column - head * rows, per_phase, batch_rows)

    key_index = lax.broadcasted_iota(jnp.int32, (old, tall), 0)
    key_patch = patch_of(key_index, micro_count, batch_rows)
    row_patch = row_patch_of(lax.broadcasted_iota(jnp.int32, (old, tall), 1))
    is_text = (key_index >= img) & (key_index < img + txt)
    for f in range(phases):
        first = f * per_phase
        seen = (key_patch < first) | (key_patch > row_patch + first)
        mask_old[f] = jnp.where(is_text | ((key_index < img) & seen), 1.0, 0.0)
    key_patch = patch_of(
        lax.broadcasted_iota(jnp.int32, (rows, tall), 0), per_phase, batch_rows
    )
    row_patch = row_patch_of(lax.broadcasted_iota(jnp.int32, (rows, tall), 1))
    mask_new[...] = jnp.where(key_patch <= row_patch, 1.0, 0.0)
    row_head = patch_of(lax.broadcasted_iota(jnp.int32, head_mask.shape, 0), group_heads, rows)
    feature = lax.broadcasted_iota(jnp.int32, head_mask.shape, 1)
    feature_head = patch_of(feature, group_heads, HEAD_DIM)
    head_mask[...] = jnp.where(row_head == feature_head, 1.0, 0.0)
    turned_mask = head_mask[...].T

    for q in range(patches):

        @pl.when(p == q)
        def _():
            gate[...] = mod_ref[2:3, q * columns : (q + 1) * columns]

    @pl.loop(0, groups)
    def _(g):
        keys[g, img:] = jnp.zeros((old - img, group_inner), BF16)
        values[g, img:] = jnp.zeros((old - img, group_inner), BF16)
        for j in range(group_heads):
            own = slice(j * HEAD_DIM, (j + 1) * HEAD_DIM)
            for source, start, count in ((stale_ref, 0, img), (text_ref, img, txt)):
                pair = source[g * group_heads + j].astype(F32)
                key = pair[:, :HEAD_DIM]
                scale = lax.rsqrt(jnp.mean(key * key, axis=-1, keepdims=True) + EPS_NORM)
                keys[g, start : start + count, own] = (key * scale).astype(BF16)
                values[g, start : start + count, own] = pair[:, HEAD_DIM:].astype(BF16)

    for g in range(groups):
        for c in range(3):
            weight_copy(c, g).wait()

    def out_ready():
        out_copy.wait()
        if out_turned:
            for g in range(patches * groups):
                part = slice(g * group_inner, (g + 1) * group_inner)
                w_back[part] = w_out[:, part].T

    @pl.when(s > 0)
    def _():
        out_ready()

    def att_copy(f, g, q):
        return pltpu.make_async_remote_copy(
            src_ref=att_all.at[f, p, g], dst_ref=att_all.at[f, p, g], send_sem=a_send.at[f, q, g],
            recv_sem=a_recv.at[f, p, g], device_id={"patch": q}, device_id_type=MESH,
        )

    def att_arrival(f, g, q):
        return pltpu.make_async_remote_copy(
            src_ref=att_all.at[f, q, g], dst_ref=att_all.at[f, q, g], send_sem=a_send.at[f, q, g],
            recv_sem=a_recv.at[f, q, g], device_id={"patch": q}, device_id_type=MESH,
        )

    def out_part(f, q, g):
        start = pl.multiple_of(q * (groups * group_inner) + g * group_inner, group_inner)
        source = w_back if out_turned else w_out
        return jnp.dot(
            att_all[f, q, g], source[pl.ds(start, group_inner)], preferred_element_type=F32
        )

    @pl.loop(0, phases)
    def _(f):
        for q in range(patches):

            @pl.when((s > 0) | (p != q))
            def _():
                x_arrival(f, q).wait_recv()

        for q in range(patches):
            xfull[:, q * columns : (q + 1) * columns] = xbuf[f, q].astype(F32)
        x = xfull[...]
        centred = x - jnp.mean(x, axis=-1, keepdims=True)
        var = jnp.mean(centred * centred, axis=-1, keepdims=True)
        unit = centred * lax.rsqrt(var + EPS_NORM)
        unit = (unit * (1.0 + mod_ref[1:2]) + mod_ref[0:1]).astype(BF16)
        for j in range(group_heads):
            normed[j * rows : (j + 1) * rows] = unit
        own_rows = pl.ds(pl.multiple_of(f * rows, rows), rows)

        def project(g):
            part = slice(g * group_inner, (g + 1) * group_inner)
            turned = []
            for c in range(2):
                product = lax.dot_general(
                    w_qkv[c, part], normed[...] if c == 0 else normed[:rows],
                    (((1,), (1,)), ((), ())), preferred_element_type=F32,
                )
                turned.append(product.astype(BF16))
            value = lax.dot_general(
                normed[:rows], w_qkv[2, part], (((1,), (1,)), ((), ())), preferred_element_type=F32
            )
            return turned[0], turned[1], value.astype(BF16)

        def unit_heads(turned):
            product = turned.astype(F32).reshape(group_heads, HEAD_DIM, turned.shape[-1])
            scale = lax.rsqrt(jnp.mean(product * product, axis=1, keepdims=True) + EPS_NORM)
            return (product * scale).astype(BF16).astype(F32).reshape(turned.shape)

        def attend(g, query, key, value):
            key = unit_heads(key).T.astype(BF16)
            query = (unit_heads(query) * (turned_mask * HEAD_DIM**-0.5)).astype(BF16)
            power_old = jnp.exp(jnp.dot(keys[g], query, preferred_element_type=F32)) * mask_old[f]
            power_new = jnp.exp(jnp.dot(key, query, preferred_element_type=F32)) * mask_new[...]
            total = jnp.sum(power_old, axis=0, keepdims=True) + jnp.sum(
                power_new, axis=0, keepdims=True
            )
            share = 1.0 / total
            att = lax.dot_general(
                (power_old * share).astype(BF16), values[g], (((0,), (0,)), ((), ())),
                preferred_element_type=F32,
            )
            att += lax.dot_general(
                (power_new * share).astype(BF16), value, (((0,), (0,)), ((), ())),
                preferred_element_type=F32,
            )
            att = (att * head_mask[...]).reshape(group_heads, rows, group_inner)
            att_all[f, p, g] = jnp.sum(att, axis=0).astype(BF16)
            for q in others:
                att_copy(f, g, q).start()
            return key, value

        ahead = project(0)
        fresh = []
        for g in range(groups):
            now = ahead
            if g + 1 < groups:
                ahead = project(g + 1)
            fresh.append(attend(g, *now))

        @pl.when((s == 0) & (f == 0))
        def _():
            out_ready()

        for g in range(groups):
            keys[g, own_rows], values[g, own_rows] = fresh[g]
        update = out_part(f, p, 0)
        for g in range(1, groups):
            update += out_part(f, p, g)
        for g in range(groups):
            for q in others:
                att_arrival(f, g, q).wait_recv()
                update += out_part(f, q, g)
        newx[f] = (xbuf[f, p].astype(F32) + gate[...] * update).astype(BF16)

        @pl.when(s < last)
        def _():
            for q in range(patches):
                x_copy(newx, f, q, x_send, {"section": s + 1, "patch": q}).start()

    def v_copy(e, q):
        return pltpu.make_async_remote_copy(
            src_ref=speed.at[pl.ds(e * half, half), q], dst_ref=speeds.at[b, p],
            send_sem=v_send.at[e, q], recv_sem=v_recv.at[b, p],
            device_id={"cfg": e, "patch": q}, device_id_type=MESH,
        )

    def v_arrival(e, q):
        return pltpu.make_async_remote_copy(
            src_ref=speed.at[pl.ds(0, half), q], dst_ref=speeds.at[e, q],
            send_sem=v_send.at[e, q], recv_sem=v_recv.at[e, q],
            device_id={"cfg": e, "patch": q}, device_id_type=MESH,
        )

    def g_copy(t):
        return pltpu.make_async_remote_copy(
            src_ref=guided, dst_ref=guided, send_sem=g_send.at[t], recv_sem=g_recv,
            device_id={"section": t}, device_id_type=MESH,
        )

    @pl.when(s == last)
    def _():
        partial = lax.dot_general(
            newx[...].reshape(phases * rows, columns), w_final_ref[...], (((1,), (1,)), ((), ())), preferred_element_type=F32
        )
        speed[...] = partial.reshape(speed.shape)
        peers = []
        for e in range(branches):
            for d in range(patches):
                if e or d:
                    peers.append((lax.rem(b + e, branches), lax.rem(p + d, patches)))
        for e, q in peers:
            v_copy(e, q).start()
        speeds[b, p] = speed[pl.ds(b * half, half), p]
        for e, q in peers:
            v_arrival(e, q).wait_recv()
        conditional = jnp.sum(speeds[0], axis=0)
        unconditional = jnp.sum(speeds[1], axis=0)
        guided[...] = unconditional + guide_ref[0] * (conditional - unconditional)
        for t in range(last):
            g_copy(t).start()
        for e, q in peers:
            v_copy(e, q).wait_send()
        for t in range(last):
            g_copy(t).wait_send()

    @pl.loop(0, phases)
    def _(f):
        @pl.when(s == 0)
        def _():
            for q in others:
                embed_copy(f, q).wait_send()

        for g in range(groups):
            for q in others:
                att_copy(f, g, q).wait_send()

        @pl.when(s < last)
        def _():
            for q in range(patches):
                x_copy(newx, f, q, x_send, {"section": s + 1, "patch": q}).wait_send()

    @pl.when(s < last)
    def _():
        g_copy(s).wait_recv()

    out_ref[...] = guided[...]


def on_device(
    latent, w_in, modulation, w_qkv, text_kv, stale_kv, w_out, w_final, guidance, step_index
):
    branches, sections = lax.axis_size("cfg"), lax.axis_size("section")
    patches = lax.axis_size("patch")
    b, s, p = lax.axis_index("cfg"), lax.axis_index("section"), lax.axis_index("patch")
    micro_count, batch_rows, chan = latent.shape
    rows = micro_count * batch_rows
    own_rows = batch_rows // patches
    columns = w_in.shape[1]
    width = columns * patches
    local_inner = w_qkv.shape[2]
    heads = local_inner // HEAD_DIM
    inner = w_out.shape[1]
    txt, img = text_kv.shape[2], stale_kv.shape[2]
    old = -(-(txt + img) // 16) * 16
    half = micro_count // branches
    groups = next(g for g in (3, 2, 1) if g == 1 or local_inner % (g * 128) == 0)
    group_inner = local_inner // groups
    per_phase = 2 if micro_count % 2 == 0 else 1
    phases = micro_count // per_phase
    phase_rows = per_phase * batch_rows
    tall = heads // groups * phase_rows

    text = jnp.transpose(text_kv[0, 0], (1, 0, 2))
    stale = jnp.transpose(stale_kv[0, 0], (1, 0, 2))
    out_turned = group_inner % 128 == 0
    dims = (
        branches, sections, patches, groups, micro_count, batch_rows, img, txt, out_turned
    )
    vmem = pl.BlockSpec(memory_space=pltpu.VMEM)
    dma = pltpu.SemaphoreType.DMA
    guided = pl.pallas_call(
        functools.partial(kernel, dims),
        out_shape=jax.ShapeDtypeStruct((half, own_rows, chan), F32),
        in_specs=[vmem] * 6
        + [pl.BlockSpec(memory_space=pltpu.SMEM)]
        + [pl.BlockSpec(memory_space=pl.ANY)] * 2,
        out_specs=vmem,
        scratch_shapes=[
            pltpu.VMEM((3, local_inner, width), BF16),
            pltpu.VMEM((columns, inner) if out_turned else (inner, columns), BF16),
            pltpu.VMEM((inner, columns) if out_turned else (16, 128), BF16),
            pltpu.VMEM((1, columns), F32),
            pltpu.VMEM((phases, patches, phase_rows, columns), BF16),
            pltpu.VMEM((phase_rows, width), F32),
            pltpu.VMEM((tall, width), BF16),
            pltpu.VMEM((groups, old, group_inner), BF16),
            pltpu.VMEM((groups, old, group_inner), BF16),
            pltpu.VMEM((phases, old, tall), F32),
            pltpu.VMEM((phase_rows, tall), F32),
            pltpu.VMEM((tall, group_inner), F32),
            pltpu.VMEM((phases, patches, groups, phase_rows, group_inner), BF16),
            pltpu.VMEM((phases, phase_rows, columns), BF16),
            pltpu.VMEM((micro_count, patches, own_rows, chan), F32),
            pltpu.VMEM((branches, patches, half, own_rows, chan), F32),
            pltpu.VMEM((half, own_rows, chan), F32),
            dma((3, groups)),
            dma,
            dma((phases, patches)),
            dma((phases, patches)),
            dma((phases, patches)),
            dma((phases, patches, groups)),
            dma((phases, patches, groups)),
            dma((branches, patches)),
            dma((branches, patches)),
            dma((sections,)),
            dma,
        ],
        compiler_params=pltpu.CompilerParams(
            collective_id=0, has_side_effects=True, vmem_limit_bytes=60 * 1024 * 1024
        ),
    )(
        latent.astype(BF16).reshape(rows, chan), w_in, modulation[0, 0], text, stale, w_final.T,
        guidance,
        w_qkv[0], w_out[0].T if out_turned else w_out[0],
    )

    section_width = half * chan // sections
    flat_guided = jnp.transpose(guided, (1, 0, 2)).reshape(own_rows, half * chan)
    own_latent = lax.dynamic_slice(
        latent, (b * half, p * own_rows, 0), (half, own_rows, chan)
    )
    flat_latent = jnp.transpose(own_latent, (1, 0, 2)).reshape(own_rows, half * chan)
    step_size = sigma_at(step_index[0] + 1) - sigma_at(step_index[0])
    result = flat_latent + step_size * flat_guided
    return lax.dynamic_slice_in_dim(result, s * section_width, section_width, 1)


def solution(mesh):
    in_specs = (
        P(),
        P(None, "patch"),
        P("section", "cfg", None, None),
        P("section", None, "patch", None),
        P("section", "cfg", None, "patch", None),
        P("section", "cfg", None, "patch", None),
        P("section", None, "patch"),
        P("patch", None),
        P(),
        P(),
    )
    out_specs = P("patch", ("cfg", "section"))
    return jax.shard_map(
        on_device, mesh=mesh, in_specs=in_specs, out_specs=out_specs, check_vma=False
    )
```

```python
import functools

import jax
import jax.numpy as jnp
from jax import lax
from jax.experimental import pallas as pl
from jax.experimental.pallas import tpu as pltpu
from jax.sharding import PartitionSpec as P

HEAD_DIM = 64
STEPS = 28
SHIFT_SIGMA = 3.0
EPS_NORM = 1e-06
MESH = pl.DeviceIdType.MESH
BF16 = jnp.bfloat16
F32 = jnp.float32


def sigma_at(position):
    level = 1.0 - position.astype(F32) / STEPS
    return SHIFT_SIGMA * level / (1.0 + (SHIFT_SIGMA - 1.0) * level)


def patch_of(index, micro_count, batch_rows):
    patch = jnp.zeros_like(index)
    for m in range(1, micro_count):
        patch = patch + jnp.where(index >= m * batch_rows, 1, 0)
    return patch


def kernel(
    dims,
    latent_ref, w_in_ref, mod_ref, text_ref, stale_ref, w_final_ref, guide_ref, w_qkv_hbm, w_out_hbm,
    out_ref,
    w_qkv, w_out, w_back, gate, xbuf, xfull, normed, keys, values, mask_old, mask_new, head_mask,
    att_all, newx,
    speed, speeds, guided,
    w_sem, wo_sem, e_send, x_send, x_recv, a_send, a_recv, v_send, v_recv, g_send, g_recv,
):
    branches, sections, patches, groups, micro_count, batch_rows, img, txt, out_turned = dims
    b, s, p = lax.axis_index("cfg"), lax.axis_index("section"), lax.axis_index("patch")
    last = sections - 1
    phases, rows, columns = newx.shape
    heads = text_ref.shape[0]
    old, tall = mask_old.shape[1:]
    per_phase = micro_count // phases
    group_heads = heads // groups
    group_inner = group_heads * HEAD_DIM
    half = micro_count // branches

    def weight_copy(c, g):
        part = pl.ds(g * group_inner, group_inner)
        return pltpu.make_async_copy(w_qkv_hbm.at[c, part], w_qkv.at[c, part], w_sem.at[c, g])

    for g in range(groups):
        for c in range(3):
            weight_copy(c, g).start()
    out_copy = pltpu.make_async_copy(w_out_hbm, w_out, wo_sem)
    out_copy.start()

    others = [lax.rem(p + d, patches) for d in range(1, patches)]

    barrier = pltpu.get_barrier_semaphore()
    for q in others:
        pl.semaphore_signal(barrier, inc=1, device_id={"patch": q}, device_id_type=MESH)

    @pl.when(s > 0)
    def _():
        for q in range(patches):
            pl.semaphore_signal(
                barrier, inc=1, device_id={"section": s - 1, "patch": q}, device_id_type=MESH
            )

    @pl.when(s < last)
    def _():
        pl.semaphore_signal(barrier, inc=1, device_id={"section": last}, device_id_type=MESH)

    @pl.when(s == last)
    def _():
        for e in range(1, branches):
            for q in range(patches):
                pl.semaphore_signal(
                    barrier, inc=1, device_id={"cfg": lax.rem(b + e, branches), "patch": q},
                    device_id_type=MESH,
                )

    @pl.when(s < last)
    def _():
        pl.semaphore_wait(barrier, 2 * patches - 1)

    @pl.when(s == last)
    def _():
        pl.semaphore_wait(barrier, branches * patches - 1 + last)

    def x_copy(source, f, q, sems, target):
        return pltpu.make_async_remote_copy(
            src_ref=source.at[f], dst_ref=xbuf.at[f, p], send_sem=sems.at[f, q],
            recv_sem=x_recv.at[f, p], device_id=target, device_id_type=MESH,
        )

    def embed_copy(f, q):
        return pltpu.make_async_remote_copy(
            src_ref=xbuf.at[f, p], dst_ref=xbuf.at[f, p], send_sem=e_send.at[f, q],
            recv_sem=x_recv.at[f, p], device_id={"patch": q}, device_id_type=MESH,
        )

    def x_arrival(f, q):
        return pltpu.make_async_remote_copy(
            src_ref=newx.at[f], dst_ref=xbuf.at[f, q], send_sem=x_send.at[f, 0],
            recv_sem=x_recv.at[f, q], device_id={"patch": others[0]}, device_id_type=MESH,
        )

    @pl.when(s == 0)
    def _():
        start = latent_ref[...].astype(BF16).reshape(phases * rows, latent_ref.shape[2])
        embedded = jnp.dot(start, w_in_ref[...], preferred_element_type=F32)
        embedded = embedded.astype(BF16).reshape(phases, rows, columns)
        for f in range(phases):
            xbuf[f, p] = embedded[f]
            for q in others:
                embed_copy(f, q).start()

    def row_patch_of(column):
        head = patch_of(column, group_heads, rows)
        return patch_of(column - head * rows, per_phase, batch_rows)

    key_index = lax.broadcasted_iota(jnp.int32, (old, tall), 0)
    key_patch = patch_of(key_index, micro_count, batch_rows)
    row_patch = row_patch_of(lax.broadcasted_iota(jnp.int32, (old, tall), 1))
    is_text = (key_index >= img) & (key_index < img + txt)
    for f in range(phases):
        first = f * per_phase
        seen = (key_patch < first) | (key_patch > row_patch + first)
        mask_old[f] = jnp.where(is_text | ((key_index < img) & seen), 1.0, 0.0)
    key_patch = patch_of(
        lax.broadcasted_iota(jnp.int32, (rows, tall), 0), per_phase, batch_rows
    )
    row_patch = row_patch_of(lax.broadcasted_iota(jnp.int32, (rows, tall), 1))
    mask_new[...] = jnp.where(key_patch <= row_patch, 1.0, 0.0)
    row_head = patch_of(lax.broadcasted_iota(jnp.int32, head_mask.shape, 0), group_heads, rows)
    feature = lax.broadcasted_iota(jnp.int32, head_mask.shape, 1)
    feature_head = patch_of(feature, group_heads, HEAD_DIM)
    head_mask[...] = jnp.where(row_head == feature_head, 1.0, 0.0)
    turned_mask = head_mask[...].T

    for q in range(patches):

        @pl.when(p == q)
        def _():
            gate[...] = mod_ref[2, :, q * columns : (q + 1) * columns]

    @pl.loop(0, groups)
    def _(g):
        keys[g, img:] = jnp.zeros((old - img, group_inner), BF16)
        values[g, img:] = jnp.zeros((old - img, group_inner), BF16)
        for j in range(group_heads):
            own = slice(j * HEAD_DIM, (j + 1) * HEAD_DIM)
            for source, start, count in ((stale_ref, 0, img), (text_ref, img, txt)):
                pair = source[g * group_heads + j].astype(F32)
                key = pair[:, :HEAD_DIM]
                scale = lax.rsqrt(jnp.mean(key * key, axis=-1, keepdims=True) + EPS_NORM)
                keys[g, start : start + count, own] = (key * scale).astype(BF16)
                values[g, start : start + count, own] = pair[:, HEAD_DIM:].astype(BF16)

    for g in range(groups):
        for c in range(3):
            weight_copy(c, g).wait()

    def out_ready():
        out_copy.wait()
        if out_turned:
            for g in range(patches * groups):
                part = slice(g * group_inner, (g + 1) * group_inner)
                w_back[part] = w_out[:, part].T

    @pl.when(s > 0)
    def _():
        out_ready()

    def att_copy(f, g, q):
        return pltpu.make_async_remote_copy(
            src_ref=att_all.at[f, p, g], dst_ref=att_all.at[f, p, g], send_sem=a_send.at[f, q, g],
            recv_sem=a_recv.at[f, p, g], device_id={"patch": q}, device_id_type=MESH,
        )

    def att_arrival(f, g, q):
        return pltpu.make_async_remote_copy(
            src_ref=att_all.at[f, q, g], dst_ref=att_all.at[f, q, g], send_sem=a_send.at[f, q, g],
            recv_sem=a_recv.at[f, q, g], device_id={"patch": q}, device_id_type=MESH,
        )

    def out_part(f, q, g):
        start = pl.multiple_of(q * (groups * group_inner) + g * group_inner, group_inner)
        source = w_back if out_turned else w_out
        return jnp.dot(
            att_all[f, q, g], source[pl.ds(start, group_inner)], preferred_element_type=F32
        )

    @pl.loop(0, phases)
    def _(f):
        for q in range(patches):

            @pl.when((s > 0) | (p != q))
            def _():
                x_arrival(f, q).wait_recv()

        for q in range(patches):
            xfull[:, q * columns : (q + 1) * columns] = xbuf[f, q].astype(F32)
        x = xfull[...]
        centred = x - jnp.mean(x, axis=-1, keepdims=True)
        var = jnp.mean(centred * centred, axis=-1, keepdims=True)
        unit = centred * lax.rsqrt(var + EPS_NORM)
        unit = (unit * (1.0 + mod_ref[1]) + mod_ref[0]).astype(BF16)
        for j in range(group_heads):
            normed[j * rows : (j + 1) * rows] = unit
        own_rows = pl.ds(pl.multiple_of(f * rows, rows), rows)

        def project(g):
            part = slice(g * group_inner, (g + 1) * group_inner)
            turned = []
            for c in range(2):
                product = lax.dot_general(
                    w_qkv[c, part], normed[...] if c == 0 else normed[:rows],
                    (((1,), (1,)), ((), ())), preferred_element_type=F32,
                )
                turned.append(product.astype(BF16))
            value = lax.dot_general(
                normed[:rows], w_qkv[2, part], (((1,), (1,)), ((), ())), preferred_element_type=F32
            )
            return turned[0], turned[1], value.astype(BF16)

        def unit_heads(turned):
            product = turned.astype(F32).reshape(group_heads, HEAD_DIM, turned.shape[-1])
            scale = lax.rsqrt(jnp.mean(product * product, axis=1, keepdims=True) + EPS_NORM)
            return (product * scale).astype(BF16).astype(F32).reshape(turned.shape)

        def attend(g, query, key, value):
            key = unit_heads(key).T.astype(BF16)
            query = (unit_heads(query) * (turned_mask * HEAD_DIM**-0.5)).astype(BF16)
            power_old = jnp.exp(jnp.dot(keys[g], query, preferred_element_type=F32)) * mask_old[f]
            power_new = jnp.exp(jnp.dot(key, query, preferred_element_type=F32)) * mask_new[...]
            total = jnp.sum(power_old, axis=0, keepdims=True) + jnp.sum(
                power_new, axis=0, keepdims=True
            )
            share = 1.0 / total
            att = lax.dot_general(
                (power_old * share).astype(BF16), values[g], (((0,), (0,)), ((), ())),
                preferred_element_type=F32,
            )
            att += lax.dot_general(
                (power_new * share).astype(BF16), value, (((0,), (0,)), ((), ())),
                preferred_element_type=F32,
            )
            att = (att * head_mask[...]).reshape(group_heads, rows, group_inner)
            att_all[f, p, g] = jnp.sum(att, axis=0).astype(BF16)
            for q in others:
                att_copy(f, g, q).start()
            return key, value

        ahead = project(0)
        fresh = []
        for g in range(groups):
            now = ahead
            if g + 1 < groups:
                ahead = project(g + 1)
            fresh.append(attend(g, *now))

        @pl.when((s == 0) & (f == 0))
        def _():
            out_ready()

        for g in range(groups):
            keys[g, own_rows], values[g, own_rows] = fresh[g]
        update = out_part(f, p, 0)
        for g in range(1, groups):
            update += out_part(f, p, g)
        for g in range(groups):
            for q in others:
                att_arrival(f, g, q).wait_recv()
                update += out_part(f, q, g)
        newx[f] = (xbuf[f, p].astype(F32) + gate[...] * update).astype(BF16)

        @pl.when(s < last)
        def _():
            for q in range(patches):
                x_copy(newx, f, q, x_send, {"section": s + 1, "patch": q}).start()

    def v_copy(e, q):
        return pltpu.make_async_remote_copy(
            src_ref=speed.at[pl.ds(e * half, half), q], dst_ref=speeds.at[b, p],
            send_sem=v_send.at[e, q], recv_sem=v_recv.at[b, p],
            device_id={"cfg": e, "patch": q}, device_id_type=MESH,
        )

    def v_arrival(e, q):
        return pltpu.make_async_remote_copy(
            src_ref=speed.at[pl.ds(0, half), q], dst_ref=speeds.at[e, q],
            send_sem=v_send.at[e, q], recv_sem=v_recv.at[e, q],
            device_id={"cfg": e, "patch": q}, device_id_type=MESH,
        )

    def g_copy(t):
        return pltpu.make_async_remote_copy(
            src_ref=guided, dst_ref=guided, send_sem=g_send.at[t], recv_sem=g_recv,
            device_id={"section": t}, device_id_type=MESH,
        )

    @pl.when(s == last)
    def _():
        partial = lax.dot_general(
            newx[...].reshape(phases * rows, columns), w_final_ref[...], (((1,), (1,)), ((), ())), preferred_element_type=F32
        )
        speed[...] = partial.reshape(speed.shape)
        peers = []
        for e in range(branches):
            for d in range(patches):
                if e or d:
                    peers.append((lax.rem(b + e, branches), lax.rem(p + d, patches)))
        for e, q in peers:
            v_copy(e, q).start()
        speeds[b, p] = speed[pl.ds(b * half, half), p]
        for e, q in peers:
            v_arrival(e, q).wait_recv()
        conditional = jnp.sum(speeds[0], axis=0)
        unconditional = jnp.sum(speeds[1], axis=0)
        guided[...] = unconditional + guide_ref[0] * (conditional - unconditional)
        for t in range(last):
            g_copy(t).start()
        for e, q in peers:
            v_copy(e, q).wait_send()
        for t in range(last):
            g_copy(t).wait_send()

    @pl.loop(0, phases)
    def _(f):
        @pl.when(s == 0)
        def _():
            for q in others:
                embed_copy(f, q).wait_send()

        for g in range(groups):
            for q in others:
                att_copy(f, g, q).wait_send()

        @pl.when(s < last)
        def _():
            for q in range(patches):
                x_copy(newx, f, q, x_send, {"section": s + 1, "patch": q}).wait_send()

    @pl.when(s < last)
    def _():
        g_copy(s).wait_recv()

    out_ref[...] = guided[...]


def on_device(
    latent, w_in, modulation, w_qkv, text_kv, stale_kv, w_out, w_final, guidance, step_index
):
    branches, sections = lax.axis_size("cfg"), lax.axis_size("section")
    patches = lax.axis_size("patch")
    b, s, p = lax.axis_index("cfg"), lax.axis_index("section"), lax.axis_index("patch")
    micro_count, batch_rows, chan = latent.shape
    own_rows = batch_rows // patches
    columns = w_in.shape[1]
    width = columns * patches
    local_inner = w_qkv.shape[2]
    heads = local_inner // HEAD_DIM
    inner = w_out.shape[1]
    txt, img = text_kv.shape[2], stale_kv.shape[2]
    old = -(-(txt + img) // 16) * 16
    half = micro_count // branches
    groups = next(g for g in (3, 2, 1) if g == 1 or local_inner % (g * 128) == 0)
    group_inner = local_inner // groups
    per_phase = 2 if micro_count % 2 == 0 else 1
    phases = micro_count // per_phase
    phase_rows = per_phase * batch_rows
    tall = heads // groups * phase_rows

    text = jnp.transpose(text_kv[0, 0], (1, 0, 2))
    stale = jnp.transpose(stale_kv[0, 0], (1, 0, 2))
    out_turned = group_inner % 128 == 0
    dims = (
        branches, sections, patches, groups, micro_count, batch_rows, img, txt, out_turned
    )
    vmem = pl.BlockSpec(memory_space=pltpu.VMEM)
    dma = pltpu.SemaphoreType.DMA
    guided = pl.pallas_call(
        functools.partial(kernel, dims),
        out_shape=jax.ShapeDtypeStruct((half, own_rows, chan), F32),
        in_specs=[vmem] * 6
        + [pl.BlockSpec(memory_space=pltpu.SMEM)]
        + [pl.BlockSpec(memory_space=pl.ANY)] * 2,
        out_specs=vmem,
        scratch_shapes=[
            pltpu.VMEM((3, local_inner, width), BF16),
            pltpu.VMEM((columns, inner) if out_turned else (inner, columns), BF16),
            pltpu.VMEM((inner, columns) if out_turned else (16, 128), BF16),
            pltpu.VMEM((1, columns), F32),
            pltpu.VMEM((phases, patches, phase_rows, columns), BF16),
            pltpu.VMEM((phase_rows, width), F32),
            pltpu.VMEM((tall, width), BF16),
            pltpu.VMEM((groups, old, group_inner), BF16),
            pltpu.VMEM((groups, old, group_inner), BF16),
            pltpu.VMEM((phases, old, tall), F32),
            pltpu.VMEM((phase_rows, tall), F32),
            pltpu.VMEM((tall, group_inner), F32),
            pltpu.VMEM((phases, patches, groups, phase_rows, group_inner), BF16),
            pltpu.VMEM((phases, phase_rows, columns), BF16),
            pltpu.VMEM((micro_count, patches, own_rows, chan), F32),
            pltpu.VMEM((branches, patches, half, own_rows, chan), F32),
            pltpu.VMEM((half, own_rows, chan), F32),
            dma((3, groups)),
            dma,
            dma((phases, patches)),
            dma((phases, patches)),
            dma((phases, patches)),
            dma((phases, patches, groups)),
            dma((phases, patches, groups)),
            dma((branches, patches)),
            dma((branches, patches)),
            dma((sections,)),
            dma,
        ],
        compiler_params=pltpu.CompilerParams(
            collective_id=0, has_side_effects=True, vmem_limit_bytes=60 * 1024 * 1024
        ),
    )(
        latent, w_in, modulation.reshape(3, 1, width), text, stale, w_final.T,
        guidance,
        w_qkv[0], w_out[0].T if out_turned else w_out[0],
    )

    section_width = half * chan // sections
    step_size = sigma_at(step_index[0] + 1) - sigma_at(step_index[0])
    if chan % section_width:
        flat = jnp.transpose(guided, (1, 0, 2)).reshape(own_rows, half * chan)
        own_latent = lax.dynamic_slice(
            latent, (b * half, p * own_rows, 0), (half, own_rows, chan)
        )
        flat_latent = jnp.transpose(own_latent, (1, 0, 2)).reshape(own_rows, half * chan)
        result = flat_latent + step_size * flat
        return lax.dynamic_slice_in_dim(result, s * section_width, section_width, 1)
    m, column = s * section_width // chan, s * section_width % chan
    size = (1, own_rows, section_width)
    own_latent = lax.dynamic_slice(latent, (b * half + m, p * own_rows, column), size)
    return (own_latent + step_size * lax.dynamic_slice(guided, (m, 0, column), size))[0]


def solution(mesh):
    in_specs = (
        P(),
        P(None, "patch"),
        P("section", "cfg", None, None),
        P("section", None, "patch", None),
        P("section", "cfg", None, "patch", None),
        P("section", "cfg", None, "patch", None),
        P("section", None, "patch"),
        P("patch", None),
        P(),
        P(),
    )
    out_specs = P("patch", ("cfg", "section"))
    return jax.shard_map(
        on_device, mesh=mesh, in_specs=in_specs, out_specs=out_specs, check_vma=False
    )
```

```python
import functools

import jax
import jax.numpy as jnp
from jax import lax
from jax.experimental import pallas as pl
from jax.experimental.pallas import tpu as pltpu
from jax.sharding import PartitionSpec as P

HEAD_DIM = 64
STEPS = 28
SHIFT_SIGMA = 3.0
EPS_NORM = 1e-06
MESH = pl.DeviceIdType.MESH
BF16 = jnp.bfloat16
F32 = jnp.float32


def sigma_at(position):
    level = 1.0 - position.astype(F32) / STEPS
    return SHIFT_SIGMA * level / (1.0 + (SHIFT_SIGMA - 1.0) * level)


def patch_of(index, micro_count, batch_rows):
    patch = jnp.zeros_like(index)
    for m in range(1, micro_count):
        patch = patch + jnp.where(index >= m * batch_rows, 1, 0)
    return patch


def kernel(
    dims,
    latent_ref, w_in_ref, mod_ref, text_ref, stale_ref, w_final_ref, guide_ref, w_qkv_hbm, w_out_hbm,
    out_ref,
    w_qkv, w_out, w_back, gate, xbuf, xfull, normed, keys, values, mask_old, mask_new, head_mask,
    att_all, newx,
    speed, speeds, guided,
    w_sem, wo_sem, e_send, x_send, x_recv, a_send, a_recv, v_send, v_recv, g_send, g_recv,
):
    branches, sections, patches, groups, micro_count, batch_rows, img, txt, out_turned = dims
    b, s, p = lax.axis_index("cfg"), lax.axis_index("section"), lax.axis_index("patch")
    last = sections - 1
    phases, rows, columns = newx.shape
    heads = text_ref.shape[0]
    old, tall = mask_old.shape[1:]
    per_phase = micro_count // phases
    group_heads = heads // groups
    group_inner = group_heads * HEAD_DIM
    half = micro_count // branches

    def weight_copy(c, g):
        part = pl.ds(g * group_inner, group_inner)
        return pltpu.make_async_copy(w_qkv_hbm.at[c, part], w_qkv.at[c, part], w_sem.at[c, g])

    for g in range(groups):
        for c in range(3):
            weight_copy(c, g).start()
    out_copy = pltpu.make_async_copy(w_out_hbm, w_out, wo_sem)
    out_copy.start()

    others = [lax.rem(p + d, patches) for d in range(1, patches)]

    barrier = pltpu.get_barrier_semaphore()
    for q in others:
        pl.semaphore_signal(barrier, inc=1, device_id={"patch": q}, device_id_type=MESH)

    @pl.when(s > 0)
    def _():
        for q in range(patches):
            pl.semaphore_signal(
                barrier, inc=1, device_id={"section": s - 1, "patch": q}, device_id_type=MESH
            )

    @pl.when(s < last)
    def _():
        pl.semaphore_signal(barrier, inc=1, device_id={"section": last}, device_id_type=MESH)

    @pl.when(s == last)
    def _():
        for e in range(1, branches):
            for q in range(patches):
                pl.semaphore_signal(
                    barrier, inc=1, device_id={"cfg": lax.rem(b + e, branches), "patch": q},
                    device_id_type=MESH,
                )

    @pl.when(s < last)
    def _():
        pl.semaphore_wait(barrier, 2 * patches - 1)

    @pl.when(s == last)
    def _():
        pl.semaphore_wait(barrier, branches * patches - 1 + last)

    def x_copy(source, f, q, sems, target):
        return pltpu.make_async_remote_copy(
            src_ref=source.at[f], dst_ref=xbuf.at[f, p], send_sem=sems.at[f, q],
            recv_sem=x_recv.at[f, p], device_id=target, device_id_type=MESH,
        )

    def embed_copy(f, q):
        return pltpu.make_async_remote_copy(
            src_ref=xbuf.at[f, p], dst_ref=xbuf.at[f, p], send_sem=e_send.at[f, q],
            recv_sem=x_recv.at[f, p], device_id={"patch": q}, device_id_type=MESH,
        )

    def x_arrival(f, q):
        return pltpu.make_async_remote_copy(
            src_ref=newx.at[f], dst_ref=xbuf.at[f, q], send_sem=x_send.at[f, 0],
            recv_sem=x_recv.at[f, q], device_id={"patch": others[0]}, device_id_type=MESH,
        )

    @pl.when(s == 0)
    def _():
        start = latent_ref[...].astype(BF16).reshape(phases * rows, latent_ref.shape[2])
        embedded = jnp.dot(start, w_in_ref[...], preferred_element_type=F32)
        embedded = embedded.astype(BF16).reshape(phases, rows, columns)
        for f in range(phases):
            xbuf[f, p] = embedded[f]
            for q in others:
                embed_copy(f, q).start()

    def row_patch_of(column):
        head = patch_of(column, group_heads, rows)
        return patch_of(column - head * rows, per_phase, batch_rows)

    key_index = lax.broadcasted_iota(jnp.int32, (old, tall), 0)
    key_patch = patch_of(key_index, micro_count, batch_rows)
    row_patch = row_patch_of(lax.broadcasted_iota(jnp.int32, (old, tall), 1))
    is_text = (key_index >= img) & (key_index < img + txt)
    for f in range(phases):
        first = f * per_phase
        seen = (key_patch < first) | (key_patch > row_patch + first)
        mask_old[f] = jnp.where(is_text | ((key_index < img) & seen), 1.0, 0.0)
    key_patch = patch_of(
        lax.broadcasted_iota(jnp.int32, (rows, tall), 0), per_phase, batch_rows
    )
    row_patch = row_patch_of(lax.broadcasted_iota(jnp.int32, (rows, tall), 1))
    mask_new[...] = jnp.where(key_patch <= row_patch, 1.0, 0.0)
    row_head = patch_of(lax.broadcasted_iota(jnp.int32, head_mask.shape, 0), group_heads, rows)
    feature = lax.broadcasted_iota(jnp.int32, head_mask.shape, 1)
    feature_head = patch_of(feature, group_heads, HEAD_DIM)
    head_mask[...] = jnp.where(row_head == feature_head, 1.0, 0.0)
    turned_mask = head_mask[...].T

    for q in range(patches):

        @pl.when(p == q)
        def _():
            gate[...] = mod_ref[2, :, q * columns : (q + 1) * columns]

    @pl.loop(0, groups)
    def _(g):
        keys[g, img:] = jnp.zeros((old - img, group_inner), BF16)
        values[g, img:] = jnp.zeros((old - img, group_inner), BF16)
        for j in range(group_heads):
            own = slice(j * HEAD_DIM, (j + 1) * HEAD_DIM)
            for source, start, count in ((stale_ref, 0, img), (text_ref, img, txt)):
                pair = source[g * group_heads + j].astype(F32)
                key = pair[:, :HEAD_DIM]
                scale = lax.rsqrt(jnp.mean(key * key, axis=-1, keepdims=True) + EPS_NORM)
                keys[g, start : start + count, own] = (key * scale).astype(BF16)
                values[g, start : start + count, own] = pair[:, HEAD_DIM:].astype(BF16)

    for g in range(groups):
        for c in range(3):
            weight_copy(c, g).wait()

    def out_ready():
        out_copy.wait()
        if out_turned:
            for g in range(patches * groups):
                part = slice(g * group_inner, (g + 1) * group_inner)
                w_back[part] = w_out[:, part].T

    @pl.when(s > 0)
    def _():
        out_ready()

    def att_copy(f, g, q):
        return pltpu.make_async_remote_copy(
            src_ref=att_all.at[f, p, g], dst_ref=att_all.at[f, p, g], send_sem=a_send.at[f, q, g],
            recv_sem=a_recv.at[f, p, g], device_id={"patch": q}, device_id_type=MESH,
        )

    def att_arrival(f, g, q):
        return pltpu.make_async_remote_copy(
            src_ref=att_all.at[f, q, g], dst_ref=att_all.at[f, q, g], send_sem=a_send.at[f, q, g],
            recv_sem=a_recv.at[f, q, g], device_id={"patch": q}, device_id_type=MESH,
        )

    def out_part(f, q, g):
        start = pl.multiple_of(q * (groups * group_inner) + g * group_inner, group_inner)
        source = w_back if out_turned else w_out
        return jnp.dot(
            att_all[f, q, g], source[pl.ds(start, group_inner)], preferred_element_type=F32
        )

    @pl.loop(0, phases)
    def _(f):
        for q in range(patches):

            @pl.when((s > 0) | (p != q))
            def _():
                x_arrival(f, q).wait_recv()

        for q in range(patches):
            xfull[:, q * columns : (q + 1) * columns] = xbuf[f, q].astype(F32)
        x = xfull[...]
        centred = x - jnp.mean(x, axis=-1, keepdims=True)
        var = jnp.mean(centred * centred, axis=-1, keepdims=True)
        unit = centred * lax.rsqrt(var + EPS_NORM)
        unit = (unit * (1.0 + mod_ref[1]) + mod_ref[0]).astype(BF16)
        for j in range(group_heads):
            normed[j * rows : (j + 1) * rows] = unit
        own_rows = pl.ds(pl.multiple_of(f * rows, rows), rows)

        def project(g):
            part = slice(g * group_inner, (g + 1) * group_inner)
            turned = []
            for c in range(2):
                product = lax.dot_general(
                    w_qkv[c, part], normed[...] if c == 0 else normed[:rows],
                    (((1,), (1,)), ((), ())), preferred_element_type=F32,
                )
                turned.append(product.astype(BF16))
            value = lax.dot_general(
                normed[:rows], w_qkv[2, part], (((1,), (1,)), ((), ())), preferred_element_type=F32
            )
            return turned[0], turned[1], value.astype(BF16)

        def unit_heads(turned):
            product = turned.astype(F32).reshape(group_heads, HEAD_DIM, turned.shape[-1])
            scale = lax.rsqrt(jnp.mean(product * product, axis=1, keepdims=True) + EPS_NORM)
            return (product * scale).astype(BF16).astype(F32).reshape(turned.shape)

        def attend(g, query, key, value):
            key = unit_heads(key).T.astype(BF16)
            query = (unit_heads(query) * (turned_mask * HEAD_DIM**-0.5)).astype(BF16)
            power_old = jnp.exp(jnp.dot(keys[g], query, preferred_element_type=F32)) * mask_old[f]
            power_new = jnp.exp(jnp.dot(key, query, preferred_element_type=F32)) * mask_new[...]
            total = jnp.sum(power_old, axis=0, keepdims=True) + jnp.sum(
                power_new, axis=0, keepdims=True
            )
            share = 1.0 / total
            att = lax.dot_general(
                (power_old * share).astype(BF16), values[g], (((0,), (0,)), ((), ())),
                preferred_element_type=F32,
            )
            att += lax.dot_general(
                (power_new * share).astype(BF16), value, (((0,), (0,)), ((), ())),
                preferred_element_type=F32,
            )
            att = (att * head_mask[...]).reshape(group_heads, rows, group_inner)
            att_all[f, p, g] = jnp.sum(att, axis=0).astype(BF16)
            for q in others:
                att_copy(f, g, q).start()
            return key, value

        ahead = project(0)
        fresh = []
        for g in range(groups):
            now = ahead
            if g + 1 < groups:
                ahead = project(g + 1)
            fresh.append(attend(g, *now))

        @pl.when((s == 0) & (f == 0))
        def _():
            out_ready()

        for g in range(groups):
            keys[g, own_rows], values[g, own_rows] = fresh[g]
        update = out_part(f, p, 0)
        for g in range(1, groups):
            update += out_part(f, p, g)
        for g in range(groups):
            for q in others:
                att_arrival(f, g, q).wait_recv()
                update += out_part(f, q, g)
        newx[f] = (xbuf[f, p].astype(F32) + gate[...] * update).astype(BF16)

        @pl.when(s < last)
        def _():
            for q in others + [p]:
                x_copy(newx, f, q, x_send, {"section": s + 1, "patch": q}).start()

    def v_copy(e, q):
        return pltpu.make_async_remote_copy(
            src_ref=speed.at[pl.ds(e * half, half), q], dst_ref=speeds.at[b, p],
            send_sem=v_send.at[e, q], recv_sem=v_recv.at[b, p],
            device_id={"cfg": e, "patch": q}, device_id_type=MESH,
        )

    def v_arrival(e, q):
        return pltpu.make_async_remote_copy(
            src_ref=speed.at[pl.ds(0, half), q], dst_ref=speeds.at[e, q],
            send_sem=v_send.at[e, q], recv_sem=v_recv.at[e, q],
            device_id={"cfg": e, "patch": q}, device_id_type=MESH,
        )

    def g_copy(t):
        return pltpu.make_async_remote_copy(
            src_ref=guided, dst_ref=guided, send_sem=g_send.at[t], recv_sem=g_recv,
            device_id={"section": t}, device_id_type=MESH,
        )

    @pl.when(s == last)
    def _():
        partial = lax.dot_general(
            newx[...].reshape(phases * rows, columns), w_final_ref[...], (((1,), (1,)), ((), ())), preferred_element_type=F32
        )
        speed[...] = partial.reshape(speed.shape)
        peers = []
        for e in range(branches):
            for d in range(patches):
                if e or d:
                    peers.append((lax.rem(b + e, branches), lax.rem(p + d, patches)))
        for e, q in peers:
            v_copy(e, q).start()
        speeds[b, p] = speed[pl.ds(b * half, half), p]
        for e, q in peers:
            v_arrival(e, q).wait_recv()
        conditional = jnp.sum(speeds[0], axis=0)
        unconditional = jnp.sum(speeds[1], axis=0)
        guided[...] = unconditional + guide_ref[0] * (conditional - unconditional)
        for t in range(last):
            g_copy(t).start()
        for e, q in peers:
            v_copy(e, q).wait_send()
        for t in range(last):
            g_copy(t).wait_send()

    @pl.loop(0, phases)
    def _(f):
        @pl.when(s == 0)
        def _():
            for q in others:
                embed_copy(f, q).wait_send()

        for g in range(groups):
            for q in others:
                att_copy(f, g, q).wait_send()

        @pl.when(s < last)
        def _():
            for q in range(patches):
                x_copy(newx, f, q, x_send, {"section": s + 1, "patch": q}).wait_send()

    @pl.when(s < last)
    def _():
        g_copy(s).wait_recv()

    out_ref[...] = guided[...]


def on_device(
    latent, w_in, modulation, w_qkv, text_kv, stale_kv, w_out, w_final, guidance, step_index
):
    branches, sections = lax.axis_size("cfg"), lax.axis_size("section")
    patches = lax.axis_size("patch")
    b, s, p = lax.axis_index("cfg"), lax.axis_index("section"), lax.axis_index("patch")
    micro_count, batch_rows, chan = latent.shape
    own_rows = batch_rows // patches
    columns = w_in.shape[1]
    width = columns * patches
    local_inner = w_qkv.shape[2]
    heads = local_inner // HEAD_DIM
    inner = w_out.shape[1]
    txt, img = text_kv.shape[2], stale_kv.shape[2]
    old = -(-(txt + img) // 16) * 16
    half = micro_count // branches
    groups = next(g for g in (3, 2, 1) if g == 1 or local_inner % (g * 128) == 0)
    group_inner = local_inner // groups
    per_phase = 2 if micro_count % 2 == 0 else 1
    phases = micro_count // per_phase
    phase_rows = per_phase * batch_rows
    tall = heads // groups * phase_rows

    text = jnp.transpose(text_kv[0, 0], (1, 0, 2))
    stale = jnp.transpose(stale_kv[0, 0], (1, 0, 2))
    out_turned = group_inner % 128 == 0
    dims = (
        branches, sections, patches, groups, micro_count, batch_rows, img, txt, out_turned
    )
    vmem = pl.BlockSpec(memory_space=pltpu.VMEM)
    dma = pltpu.SemaphoreType.DMA
    guided = pl.pallas_call(
        functools.partial(kernel, dims),
        out_shape=jax.ShapeDtypeStruct((half, own_rows, chan), F32),
        in_specs=[vmem] * 6
        + [pl.BlockSpec(memory_space=pltpu.SMEM)]
        + [pl.BlockSpec(memory_space=pl.ANY)] * 2,
        out_specs=vmem,
        scratch_shapes=[
            pltpu.VMEM((3, local_inner, width), BF16),
            pltpu.VMEM((columns, inner) if out_turned else (inner, columns), BF16),
            pltpu.VMEM((inner, columns) if out_turned else (16, 128), BF16),
            pltpu.VMEM((1, columns), F32),
            pltpu.VMEM((phases, patches, phase_rows, columns), BF16),
            pltpu.VMEM((phase_rows, width), F32),
            pltpu.VMEM((tall, width), BF16),
            pltpu.VMEM((groups, old, group_inner), BF16),
            pltpu.VMEM((groups, old, group_inner), BF16),
            pltpu.VMEM((phases, old, tall), F32),
            pltpu.VMEM((phase_rows, tall), F32),
            pltpu.VMEM((tall, group_inner), F32),
            pltpu.VMEM((phases, patches, groups, phase_rows, group_inner), BF16),
            pltpu.VMEM((phases, phase_rows, columns), BF16),
            pltpu.VMEM((micro_count, patches, own_rows, chan), F32),
            pltpu.VMEM((branches, patches, half, own_rows, chan), F32),
            pltpu.VMEM((half, own_rows, chan), F32),
            dma((3, groups)),
            dma,
            dma((phases, patches)),
            dma((phases, patches)),
            dma((phases, patches)),
            dma((phases, patches, groups)),
            dma((phases, patches, groups)),
            dma((branches, patches)),
            dma((branches, patches)),
            dma((sections,)),
            dma,
        ],
        compiler_params=pltpu.CompilerParams(
            collective_id=0, has_side_effects=True, vmem_limit_bytes=60 * 1024 * 1024
        ),
    )(
        latent, w_in, modulation.reshape(3, 1, width), text, stale, w_final.T,
        guidance,
        w_qkv[0], w_out[0].T if out_turned else w_out[0],
    )

    section_width = half * chan // sections
    step_size = sigma_at(step_index[0] + 1) - sigma_at(step_index[0])
    if chan % section_width:
        flat = jnp.transpose(guided, (1, 0, 2)).reshape(own_rows, half * chan)
        own_latent = lax.dynamic_slice(
            latent, (b * half, p * own_rows, 0), (half, own_rows, chan)
        )
        flat_latent = jnp.transpose(own_latent, (1, 0, 2)).reshape(own_rows, half * chan)
        result = flat_latent + step_size * flat
        return lax.dynamic_slice_in_dim(result, s * section_width, section_width, 1)
    m, column = s * section_width // chan, s * section_width % chan
    size = (1, own_rows, section_width)
    own_latent = lax.dynamic_slice(latent, (b * half + m, p * own_rows, column), size)
    return (own_latent + step_size * lax.dynamic_slice(guided, (m, 0, column), size))[0]


def solution(mesh):
    in_specs = (
        P(),
        P(None, "patch"),
        P("section", "cfg", None, None),
        P("section", None, "patch", None),
        P("section", "cfg", None, "patch", None),
        P("section", "cfg", None, "patch", None),
        P("section", None, "patch"),
        P("patch", None),
        P(),
        P(),
    )
    out_specs = P("patch", ("cfg", "section"))
    return jax.shard_map(
        on_device, mesh=mesh, in_specs=in_specs, out_specs=out_specs, check_vma=False
    )
```
